256 devices in a mesh: blk: 8 (over y, x_hi), group: 32 (over z, x_lo, core).
Axes of the slice: x: 4 (x_hi: 2, x_lo: 2; x = x_hi * 2 + x_lo), y: 4, z: 8, core: 2. Of those that a mesh axis runs over, the one named last changes fastest.
Arguments:
- img_emb: bfloat16 [16384, 1152], P(('blk', 'group')), may hold values from -6 to 6
- txt_emb: bfloat16 [16384, 1152], P(('blk', 'group')), may hold values from -6 to 6
- img_ids: int32 [16384], P(('blk', 'group')), may hold values from 0 to 1023
- txt_ids: int32 [16384], P(('blk', 'group')), may hold values from 0 to 1023
- scale_logarithm: float32 [1], replicated, may hold values from 3.7 to 4.4
- bias: float32 [1], replicated, may hold values from -4 to -2
Outputs:
- img_grad: float32 [16384, 1152], P(('blk', 'group'))
- txt_grad: float32 [16384, 1152], P(('blk', 'group'))
The draws below stay inside these ranges and needn't reach their ends.
All inputs are finite; a program needn't handle non-finite values.
Results may differ from the reference program's by a relative error of at most 0.0093.
Values may be sent and summed in bfloat16 or wider, within the bound.
A program may use at most 64 MiB of HBM per device.

```python
import jax
import jax.numpy as jnp
from jax import lax

D = 1152
PAIRS = 16384
IDS = 1024


def touch_ends(values, rng, least, high):
    place = [jax.random.randint(jax.random.fold_in(rng, axis), (), 0, length) for axis, length in enumerate(values.shape)]
    main_axis = values.shape.index(max(values.shape))
    beside = place[:main_axis] + [(place[main_axis] + 1) % values.shape[main_axis]] + place[main_axis + 1:]
    return values.at[tuple(place)].set(least).at[tuple(beside)].set(high)


def level_of(rng, shape, shards, least, top_value):
    def one(position, parts):
        steps = jax.random.uniform(jax.random.fold_in(jax.random.fold_in(rng, 6), position), (parts,), jnp.float32, least / len(shards), top_value / len(shards))
        return jnp.repeat(jnp.exp(steps), shape[position] // parts).reshape((-1,) + (1,) * (len(shape) - position - 1))

    loudness = one(*shards[0])
    for cut in shards[1:]:
        loudness = loudness * one(*cut)
    return loudness


def normal_values(key, extent, scale, reach, split=(), dtype=jnp.bfloat16):
    result = scale * jax.random.normal(key, extent, jnp.float32)
    if split:
        result = result * level_of(key, extent, split, -0.22, 0.18)
    return jnp.clip(result, -reach, reach).astype(dtype)


def setup_inputs(seed: int = 0) -> dict:
    seeds = jax.random.split(jax.random.key(seed), 7)
    img_emb = normal_values(seeds[0], (PAIRS, D), 1.0, 6.0, ((0, 256),))
    txt_emb = normal_values(seeds[1], (PAIRS, D), 1.0, 6.0, ((0, 256),))
    img_ids = touch_ends(jax.random.randint(seeds[2], (PAIRS,), 0, IDS), jax.random.fold_in(seeds[2], 1), 0, IDS - 1).astype(jnp.int32)
    txt_ids = touch_ends(jax.random.randint(seeds[3], (PAIRS,), 0, IDS), jax.random.fold_in(seeds[3], 1), 0, IDS - 1).astype(jnp.int32)
    scale_logarithm = jnp.clip(jax.random.uniform(seeds[4], (1,), jnp.float32, 3.7, 4.4), 3.7, 4.4)
    bias = jnp.clip(jax.random.uniform(seeds[5], (1,), jnp.float32, -4.0, -2.0), -4.0, -2.0)
    return {"img_emb": img_emb, "txt_emb": txt_emb, "img_ids": img_ids, "txt_ids": txt_ids, "scale_logarithm": scale_logarithm, "bias": bias}


def unit_rows(embedding):
    widened = embedding.astype(jnp.float32)
    inverse = lax.rsqrt(lax.optimization_barrier(jnp.sum(widened * widened, axis=1, keepdims=True)) + 1e-06)
    return (widened * inverse, inverse)

def norm_backward(direction, unit, inverse):
    return inverse * (direction - unit * lax.optimization_barrier(jnp.sum(unit * direction, axis=1, keepdims=True)))

def reference(img_emb, txt_emb, img_ids, txt_ids, scale_logarithm, bias):
    img_float, img_inverse = unit_rows(img_emb)
    txt_float, txt_inverse = unit_rows(txt_emb)
    img_unit = img_float.astype(jnp.bfloat16)
    text_unit_vectors = txt_float.astype(jnp.bfloat16)
    logit_scale_factor = jnp.exp(scale_logarithm[0])
    logit_bias = bias[0]
    block_rows = 512 if PAIRS % 512 == 0 else PAIRS
    block_count = PAIRS // block_rows
    image_blocks = img_unit.reshape(block_count, block_rows, D)
    label_blocks = img_ids.reshape(block_count, block_rows)

    def one_block(text_grad_sum, pieces):
        image_rows, image_labels = pieces
        pair_logits = jnp.dot(image_rows, text_unit_vectors.T, preferred_element_type=jnp.float32)
        positive_pair_mask = (image_labels[:, None] == txt_ids[None, :]).astype(jnp.float32)
        pair_multipliers = (jax.nn.sigmoid(logit_scale_factor * pair_logits + logit_bias) - positive_pair_mask).astype(jnp.bfloat16)
        image_portion = logit_scale_factor * jnp.dot(pair_multipliers, text_unit_vectors, preferred_element_type=jnp.float32)
        text_grad_sum = text_grad_sum + jnp.einsum('rt,rd->td', pair_multipliers.astype(jnp.float32), image_rows.astype(jnp.float32))
        return (text_grad_sum, image_portion)
    text_grad_sum, image_direction_grad = lax.scan(one_block, jnp.zeros((PAIRS, D), jnp.float32), (image_blocks, label_blocks))
    image_direction_grad = image_direction_grad.reshape(PAIRS, D)
    text_direction_grad = logit_scale_factor * text_grad_sum
    img_grad = norm_backward(image_direction_grad, img_float, img_inverse)
    txt_grad = norm_backward(text_direction_grad, txt_float, txt_inverse)
    return (img_grad, txt_grad)
```

```python
import functools

import jax
import jax.numpy as jnp
from jax import lax
from jax.experimental import pallas as pl
from jax.experimental.pallas import tpu as pltpu
from jax.sharding import PartitionSpec as P

MESH = pl.DeviceIdType.MESH
D = 1152
OWN = 64
HALF = 32
QUART = 16
ROWS = 1024
N_COPIES = 160

IMG_ORDER = [
    (4, 1), (4, 0),
    (3, 1), (5, 1), (3, 0), (5, 0),
    (2, 1), (6, 1), (2, 0), (6, 0),
    (1, 1), (7, 1), (0, 1), (1, 0), (7, 0), (0, 0),
]
IMG_ROW = {key: OWN * place for place, key in enumerate(IMG_ORDER)}

TXT_BASE = {
    ("A", 2): 0, ("B", 2): 128,
    ("A", 1): 256, ("A", 3): 384, ("B", 1): 512, ("B", 3): 640,
    ("A", 0): 768, ("B", 0): 896,
}


def txt_row(path, second, first):
    return TXT_BASE[path, second] + HALF * first


def unit_rows(embedding):
    widened = embedding.astype(jnp.float32)
    inverse = lax.rsqrt(jnp.sum(widened * widened, axis=1, keepdims=True) + 1e-06)
    return widened * inverse, inverse


def kernel(
    img_ref, txt_ref, ids_ref, scale_ref, bias_ref, img_out, txt_out,
    imgs, txts, img_tiles, txt_tiles, img_col, txt_line, coef, coef_t, img_part, txt_part,
    t1_send, t1_recv, t2_send, t2_recv, t3_send, t3_recv, t4_send, t4_recv,
    core_send, core_recv, z_send, z_recv, send_sems, recv_sems,
):
    f32, bf16 = jnp.float32, jnp.bfloat16
    blk, grp = lax.axis_index("blk"), lax.axis_index("group")
    y, x_hi = lax.div(blk, 2), lax.rem(blk, 2)
    z, x_lo, core = lax.div(grp, 4), lax.rem(lax.div(grp, 2), 2), lax.rem(grp, 2)
    x = x_hi * 2 + x_lo

    def device(dx=0, dy=0, dz=0, dc=0):
        nx, ny, nz = lax.rem(x + dx + 4, 4), lax.rem(y + dy + 4, 4), lax.rem(z + dz + 8, 8)
        nc = lax.rem(core + dc, 2)
        return (ny * 2 + lax.div(nx, 2), (nz * 2 + lax.rem(nx, 2)) * 2 + nc)

    near = {
        "x+": device(dx=1), "x-": device(dx=-1), "x2": device(dx=2),
        "y+": device(dy=1), "y-": device(dy=-1), "y2": device(dy=2),
        "z+": device(dz=1), "z-": device(dz=-1), "z+2": device(dz=2), "z-2": device(dz=-2), "z4": device(dz=4),
        "core": device(dc=1),
    }
    started = []

    def send(src, dst, to):
        number = len(started)
        copy = pltpu.make_async_remote_copy(
            src_ref=src, dst_ref=dst, send_sem=send_sems.at[number], recv_sem=recv_sems.at[number],
            device_id=near[to], device_id_type=MESH,
        )
        copy.start()
        started.append(copy)
        return copy

    barrier = pltpu.get_barrier_semaphore()
    for there in near.values():
        pl.semaphore_signal(barrier, inc=1, device_id=there, device_id_type=MESH)

    own_img, own_txt = IMG_ROW[0, 0], {p: txt_row(p, 0, 0) for p in "AB"}
    imgs[own_img:own_img + OWN, :] = unit_rows(img_ref[...])[0].astype(bf16)
    unit = unit_rows(txt_ref[...])[0].astype(bf16)
    txts[own_txt["A"]:own_txt["A"] + HALF, :] = unit[:HALF]
    txts[own_txt["B"]:own_txt["B"] + HALF, :] = unit[HALF:]
    img_tiles[0, 0] = ids_ref[0]
    txt_tiles[0, 0] = ids_ref[1]
    pl.semaphore_wait(barrier, len(near))

    first_axis, second_axis = {"A": "x", "B": "y"}, {"A": "y", "B": "x"}

    def text(path, second, first, low=0, high=HALF):
        row = txt_row(path, second, first)
        return txts.at[row + low:row + high, :]

    def image(dz, cr, low=0, high=OWN):
        row = IMG_ROW[dz, cr]
        return imgs.at[row + low:row + high, :]

    def send_text(path, src, dst, axis, way, low=0, high=HALF):
        return send(text(path, *src, low, high), text(path, *dst, low, high), axis[path] + way)

    def send_image(src, dst, way, low, high):
        return send(image(src, 0, low, high), image(dst, 0, low, high), "z" + way)

    hop = {}
    hop["idc"] = send(img_tiles.at[0, 0], img_tiles.at[0, 1], "core")
    hop["idx1"] = send(txt_tiles.at[0, 0], txt_tiles.at[0, 1], "x+")
    for p in "AB":
        hop[p, 0, 1] = send_text(p, (0, 0), (0, 1), first_axis, "+")
        hop[p, 0, 3] = send_text(p, (0, 0), (0, 3), first_axis, "-")
    for half in (0, 1):
        hop["z", 1, half] = send_image(0, 1, "+", HALF * half, HALF * half + HALF)
        hop["z", 7, half] = send_image(0, 7, "-", HALF * half, HALF * half + HALF)
    for p in "AB":
        hop[p, 1, 0] = send_text(p, (0, 0), (1, 0), second_axis, "+")
        hop[p, 3, 0] = send_text(p, (0, 0), (3, 0), second_axis, "-")
    hop["c", 0] = send(image(0, 0), image(0, 1), "core")
    hop["idc"].wait_recv()
    hop["idz1"] = send(img_tiles.at[0], img_tiles.at[1], "z+")
    hop["idx1"].wait_recv()
    hop["idx2"] = send(txt_tiles.at[0, 0:2], txt_tiles.at[0, 2:4], "x2")

    for p in "AB":
        hop[p, 0, 1].wait_recv()
        hop[p, 0, 3].wait_recv()
        hop[p, 0, 2, 0] = send_text(p, (0, 1), (0, 2), first_axis, "+", 0, QUART)
        hop[p, 0, 2, 1] = send_text(p, (0, 3), (0, 2), first_axis, "-", QUART, HALF)
        for e in (1, 3):
            hop[p, 1, e] = send_text(p, (0, e), (1, e), second_axis, "+")
            hop[p, 3, e] = send_text(p, (0, e), (3, e), second_axis, "-")

    def pass_images(k):
        for half in (0, 1):
            hop["z", k, half].wait_recv()
            if k < 3 or half == 0:
                hop["z", k + 1, half] = send_image(k, k + 1, "+", HALF * half, HALF * half + HALF)
            hop["z", 8 - k, half].wait_recv()
            if k < 3 or half == 1:
                hop["z", 7 - k, half] = send_image(8 - k, 7 - k, "-", HALF * half, HALF * half + HALF)
        for dz in (k, 8 - k):
            hop["c", dz] = send(image(dz, 0), image(dz, 1), "core")

    pass_images(1)
    hop["idz1"].wait_recv()
    hop["idz2"] = send(img_tiles.at[0:2], img_tiles.at[2:4], "z+2")
    hop["idx2"].wait_recv()
    hop["idy1"] = send(txt_tiles.at[0], txt_tiles.at[1], "y+")
    for p in "AB":
        hop[p, 1, 0].wait_recv()
        hop[p, 2, 0] = send_text(p, (1, 0), (2, 0), second_axis, "+")
        hop[p, 3, 0].wait_recv()
        hop[p, 0, 2, 0].wait_recv()
        hop[p, 0, 2, 1].wait_recv()
        hop[p, 1, 2] = send_text(p, (0, 2), (1, 2), second_axis, "+")
        hop[p, 3, 2] = send_text(p, (0, 2), (3, 2), second_axis, "-")
    for p in "AB":
        hop[p, 1, 1].wait_recv()
        hop[p, 2, 1] = send_text(p, (1, 1), (2, 1), second_axis, "+")
        hop[p, 3, 3].wait_recv()
        hop[p, 2, 3] = send_text(p, (3, 3), (2, 3), second_axis, "-")
    pass_images(2)
    hop["idz2"].wait_recv()
    hop["idz4"] = send(img_tiles.at[0:4], img_tiles.at[4:8], "z4")
    hop["idy1"].wait_recv()
    hop["idy2"] = send(txt_tiles.at[0:2], txt_tiles.at[2:4], "y2")
    for p in "AB":
        hop[p, 1, 3].wait_recv()
        hop[p, 3, 1].wait_recv()
        hop[p, 1, 2].wait_recv()
        hop[p, 3, 2].wait_recv()
        hop[p, 2, 2] = send_text(p, (3, 2), (2, 2), second_axis, "-")
    pass_images(3)
    hop["z", 4, 0].wait_recv()
    hop["z", 4, 1].wait_recv()
    hop["c", 4] = send(image(4, 0), image(4, 1), "core")

    hop["idz4"].wait_recv()
    hop["idy2"].wait_recv()
    lane = lax.broadcasted_iota(jnp.int32, (1, 128), 1)
    for (p, d), base in TXT_BASE.items():
        row = 0 if p == "A" else 1
        line = None
        for e in range(4):
            tile = (txt_tiles[d, e] if p == "A" else txt_tiles[e, d])[row:row + 1, :]
            line = tile if line is None else jnp.where(lane < HALF * e, line, tile)
        txt_line[:, base:base + 128] = line
    for place in range(0, 16, 2):
        (z0, c0), (z1, c1) = IMG_ORDER[place], IMG_ORDER[place + 1]
        line = jnp.where(lane < OWN, img_tiles[z0, c0][0:1, :], img_tiles[z1, c1][0:1, :])
        img_col[OWN * place:OWN * place + 128, :] = jnp.transpose(jnp.broadcast_to(line, (128, 128)))

    for p in "AB":
        for e in range(4):
            hop[p, 2, e].wait_recv()
    for dz in range(8):
        hop["c", dz].wait_recv()

    scale = jnp.exp(jnp.full((1, 256), scale_ref[0], f32))
    half_scale, half_bias = 0.5 * scale, jnp.full((1, 256), 0.5 * bias_ref[0], f32)

    def score_tile(step, carry):
        r = pl.multiple_of(lax.div(step, 4) * 256, 256)
        t = pl.multiple_of(lax.rem(step, 4) * 256, 256)
        scores = lax.dot_general(
            imgs[pl.ds(r, 256), :], txts[pl.ds(t, 256), :], (((1,), (1,)), ((), ())), preferred_element_type=f32
        )
        column = img_col[pl.ds(r, 256), :]
        same = jnp.concatenate([column, column], axis=1) == txt_line[:, pl.ds(t, 256)]
        value = 0.5 * jnp.tanh(half_scale * scores + half_bias) + jnp.where(same, -0.5, 0.5)
        coef[pl.ds(r, 256), pl.ds(t, 256)] = value.astype(bf16)
        coef_t[pl.ds(t, 256), pl.ds(r, 256)] = jnp.transpose(value).astype(bf16)
        return carry

    lax.fori_loop(0, 16, score_tile, 0)

    def img_terms(row, count):
        img_part[row:row + count, :] = jnp.dot(coef[row:row + count, :], txts[...], preferred_element_type=f32)

    def txt_terms(row, count):
        txt_part[row:row + count, :] = jnp.dot(coef_t[row:row + count, :], imgs[...], preferred_element_type=f32)

    def to_core(dz):
        row = IMG_ROW[dz, 1]
        core_send[OWN * dz:OWN * dz + OWN, :] = img_part[row:row + OWN, :].astype(bf16)
        hop["s", dz] = send(core_send.at[OWN * dz:OWN * dz + OWN], core_recv.at[OWN * dz:OWN * dz + OWN], "core")

    def chip_sum(dz, low=0, high=OWN):
        row = IMG_ROW[dz, 0]
        return img_part[row + low:row + high, :] + core_recv[OWN * dz + low:OWN * dz + high, :].astype(f32)

    def z_out(dz, low, high, total, way):
        rows = slice(OWN * dz + low, OWN * dz + high)
        z_send[rows, :] = total.astype(bf16)
        return send(z_send.at[rows], z_recv.at[rows], "z" + way)

    def z_step(k):
        down, up = 4 - k, 4 + k
        if k == 0:
            hop["s", 4].wait_recv()
            hop["r", 4, 0] = z_out(4, 0, HALF, chip_sum(4, 0, HALF), "-")
            hop["r", 4, 1] = z_out(4, HALF, OWN, chip_sum(4, HALF, OWN), "+")
            return
        hop["s", down].wait_recv()
        hop["s", up].wait_recv()
        for half in (0, 1):
            low, high = HALF * half, HALF * half + HALF
            for dz, before, way, lone in ((down, down + 1, "-", 1), (up, up - 1, "+", 0)):
                total = chip_sum(dz, low, high)
                if k > 1 or half != lone:
                    hop["r", before, half].wait_recv()
                    total = total + z_recv[OWN * before + low:OWN * before + high, :].astype(f32)
                hop["r", dz, half] = z_out(dz, low, high, total, way)

    def txt_far():
        for p in "AB":
            base, at = TXT_BASE[p, 2], 128 * "AB".index(p)
            t1_send[at:at + 128, :] = txt_part[base:base + 128, :].astype(bf16)
            for part, way in ((0, "-"), (1, "+")):
                rows = slice(at + OWN * part, at + OWN * part + OWN)
                hop["t1", p, part] = send(t1_send.at[rows], t1_recv.at[rows], second_axis[p] + way)

    def txt_near():
        for p in "AB":
            for part, d, way in ((0, 1, "-"), (1, 3, "+")):
                base, at = TXT_BASE[p, d], 256 * "AB".index(p) + 128 * part
                got = 128 * "AB".index(p) + OWN * part
                hop["t1", p, part].wait_recv()
                add, keep = OWN * part, OWN * (1 - part)
                t2_send[at + add:at + add + OWN, :] = (
                    txt_part[base + add:base + add + OWN, :] + t1_recv[got:got + OWN, :].astype(f32)
                ).astype(bf16)
                t2_send[at + keep:at + keep + OWN, :] = txt_part[base + keep:base + keep + OWN, :].astype(bf16)
                hop["t2", p, part] = send(
                    t2_send.at[at:at + 128], t2_recv.at[at:at + 128], second_axis[p] + way
                )

    def txt_line_sum(p, first):
        base, at = TXT_BASE[p, 0] + HALF * first, 256 * "AB".index(p) + HALF * first
        return (
            txt_part[base:base + HALF, :]
            + t2_recv[at:at + HALF, :].astype(f32)
            + t2_recv[at + 128:at + 128 + HALF, :].astype(f32)
        )

    def txt_far_first(p):
        for part in (0, 1):
            hop["t2", p, part].wait_recv()
        at = HALF * "AB".index(p)
        t3_send[at:at + HALF, :] = txt_line_sum(p, 2).astype(bf16)
        for part, way in ((0, "-"), (1, "+")):
            rows = slice(at + QUART * part, at + QUART * part + QUART)
            hop["t3", p, part] = send(t3_send.at[rows], t3_recv.at[rows], first_axis[p] + way)

    def txt_near_first(p):
        for part, first, way in ((0, 1, "-"), (1, 3, "+")):
            total = txt_line_sum(p, first)
            hop["t3", p, part].wait_recv()
            got = t3_recv[HALF * "AB".index(p) + QUART * part:HALF * "AB".index(p) + QUART * part + QUART, :].astype(f32)
            at = OWN * "AB".index(p) + HALF * part
            if part == 0:
                t4_send[at:at + QUART, :] = (total[:QUART] + got).astype(bf16)
                t4_send[at + QUART:at + HALF, :] = total[QUART:].astype(bf16)
            else:
                t4_send[at:at + QUART, :] = total[:QUART].astype(bf16)
                t4_send[at + QUART:at + HALF, :] = (total[QUART:] + got).astype(bf16)
            hop["t4", p, part] = send(t4_send.at[at:at + HALF], t4_recv.at[at:at + HALF], first_axis[p] + way)

    def finish(embedding, total):
        unit, inverse = unit_rows(embedding)
        direction = scale[:, 0:1] * total
        return inverse * (direction - unit * jnp.sum(unit * direction, axis=1, keepdims=True))

    txt_terms(0, 256)
    txt_far()
    img_terms(0, 128)
    to_core(4)
    img_terms(128, 256)
    to_core(3)
    to_core(5)
    z_step(0)
    txt_terms(256, 512)
    txt_near()
    img_terms(384, 256)
    to_core(2)
    to_core(6)
    z_step(1)
    img_terms(640, 384)
    to_core(1)
    to_core(7)
    to_core(0)
    z_step(2)
    txt_terms(768, 256)
    txt_far_first("A")
    txt_far_first("B")
    z_step(3)
    txt_near_first("A")
    txt_near_first("B")
    for p in "AB":
        low = HALF * "AB".index(p)
        total = txt_line_sum(p, 0)
        for part in (0, 1):
            hop["t4", p, part].wait_recv()
            at = OWN * "AB".index(p) + HALF * part
            total = total + t4_recv[at:at + HALF, :].astype(f32)
        txt_out[low:low + HALF, :] = finish(txt_ref[low:low + HALF, :], total)
    hop["s", 0].wait_recv()
    for half in (0, 1):
        low, high = HALF * half, HALF * half + HALF
        total = chip_sum(0, low, high)
        for dz in (1, 7):
            hop["r", dz, half].wait_recv()
            total = total + z_recv[OWN * dz + low:OWN * dz + high, :].astype(f32)
        img_out[low:high, :] = finish(img_ref[low:high, :], total)
    for copy in started:
        copy.wait_send()


def body(img_emb, txt_emb, img_ids, txt_ids, scale_logarithm, bias):
    line = jnp.stack([
        jnp.stack([jnp.tile(img_ids, 2)] * 8),
        jnp.stack([jnp.tile(txt_ids[:HALF], 4), jnp.tile(txt_ids[HALF:], 4)] * 4),
    ])
    f32, bf16, i32 = jnp.float32, jnp.bfloat16, jnp.int32
    vmem, smem = pl.BlockSpec(memory_space=pltpu.VMEM), pl.BlockSpec(memory_space=pltpu.SMEM)
    return pl.pallas_call(
        kernel,
        out_shape=(jax.ShapeDtypeStruct((OWN, D), f32), jax.ShapeDtypeStruct((OWN, D), f32)),
        in_specs=[vmem, vmem, vmem, smem, smem],
        out_specs=(vmem, vmem),
        scratch_shapes=[
            pltpu.VMEM((ROWS, D), bf16),
            pltpu.VMEM((ROWS, D), bf16),
            pltpu.VMEM((8, 2, 8, 128), i32),
            pltpu.VMEM((4, 4, 8, 128), i32),
            pltpu.VMEM((ROWS, 128), i32),
            pltpu.VMEM((1, ROWS), i32),
            pltpu.VMEM((ROWS, ROWS), bf16),
            pltpu.VMEM((ROWS, ROWS), bf16),
            pltpu.VMEM((ROWS, D), f32),
            pltpu.VMEM((ROWS, D), f32),
            pltpu.VMEM((256, D), bf16),
            pltpu.VMEM((256, D), bf16),
            pltpu.VMEM((512, D), bf16),
            pltpu.VMEM((512, D), bf16),
            pltpu.VMEM((64, D), bf16),
            pltpu.VMEM((64, D), bf16),
            pltpu.VMEM((128, D), bf16),
            pltpu.VMEM((128, D), bf16),
            pltpu.VMEM((512, D), bf16),
            pltpu.VMEM((512, D), bf16),
            pltpu.VMEM((512, D), bf16),
            pltpu.VMEM((512, D), bf16),
            pltpu.SemaphoreType.DMA((N_COPIES,)),
            pltpu.SemaphoreType.DMA((N_COPIES,)),
        ],
        compiler_params=pltpu.CompilerParams(
            collective_id=0, has_side_effects=True, vmem_limit_bytes=56 * 1024 * 1024
        ),
        cost_estimate=pl.CostEstimate(flops=7247757312, bytes_accessed=900000, transcendentals=1048576),
    )(img_emb, txt_emb, line, scale_logarithm, bias)


def solution(mesh):
    split = P(("blk", "group"), None)
    ids = P(("blk", "group"))
    return jax.shard_map(
        body,
        mesh=mesh,
        in_specs=(split, split, ids, ids, P(), P()),
        out_specs=(split, split),
        check_vma=False,
    )
```

```python
import functools

import jax
import jax.numpy as jnp
from jax import lax
from jax.experimental import pallas as pl
from jax.experimental.pallas import tpu as pltpu
from jax.sharding import PartitionSpec as P

MESH = pl.DeviceIdType.MESH
D = 1152
OWN = 64
HALF = 32
QUART = 16
ROWS = 1024
N_COPIES = 224
PIECE = 32

IMG_ORDER = [
    (4, 1), (4, 0),
    (3, 1), (5, 1), (3, 0), (5, 0),
    (2, 1), (6, 1), (2, 0), (6, 0),
    (1, 1), (7, 1), (0, 1), (1, 0), (7, 0), (0, 0),
]
IMG_ROW = {key: OWN * place for place, key in enumerate(IMG_ORDER)}

TXT_BASE = {
    ("A", 2): 0, ("B", 2): 128,
    ("A", 1): 256, ("A", 3): 384, ("B", 1): 512, ("B", 3): 640,
    ("A", 0): 768, ("B", 0): 896,
}


def txt_row(path, second, first):
    return TXT_BASE[path, second] + HALF * first


def unit_rows(embedding):
    widened = embedding.astype(jnp.float32)
    inverse = lax.rsqrt(jnp.sum(widened * widened, axis=1, keepdims=True) + 1e-06)
    return widened * inverse, inverse


def kernel(
    img_ref, txt_ref, img_ids_ref, txt_ids_ref, scale_ref, bias_ref, img_out, txt_out,
    imgs, txts, img_ids, txt_ids, img_col, txt_line, coef, img_part, txt_part,
    t1_send, t1_recv, t2_send, t2_recv, t3_send, t3_recv, t4_send, t4_recv,
    core_send, core_recv, z_send, z_recv, send_sems, recv_sems,
):
    f32, bf16 = jnp.float32, jnp.bfloat16
    blk, grp = lax.axis_index("blk"), lax.axis_index("group")
    y, x_hi = lax.div(blk, 2), lax.rem(blk, 2)
    z, x_lo, core = lax.div(grp, 4), lax.rem(lax.div(grp, 2), 2), lax.rem(grp, 2)
    x = x_hi * 2 + x_lo

    def device(dx=0, dy=0, dz=0, dc=0):
        nx, ny, nz = lax.rem(x + dx + 4, 4), lax.rem(y + dy + 4, 4), lax.rem(z + dz + 8, 8)
        nc = lax.rem(core + dc, 2)
        return (ny * 2 + lax.div(nx, 2), (nz * 2 + lax.rem(nx, 2)) * 2 + nc)

    near = {
        "x+": device(dx=1), "x-": device(dx=-1), "y+": device(dy=1), "y-": device(dy=-1),
        "z+": device(dz=1), "z-": device(dz=-1), "core": device(dc=1),
    }
    started = []
    hop = {}

    def send(key, src, dst, to):
        number = len(started)
        copy = pltpu.make_async_remote_copy(
            src_ref=src, dst_ref=dst, send_sem=send_sems.at[number], recv_sem=recv_sems.at[number],
            device_id=near[to], device_id_type=MESH,
        )
        copy.start()
        started.append(copy)
        hop[key] = copy

    barrier = pltpu.get_barrier_semaphore()
    for there in near.values():
        pl.semaphore_signal(barrier, inc=1, device_id=there, device_id_type=MESH)

    own_img, own_txt = IMG_ROW[0, 0], {p: txt_row(p, 0, 0) for p in "AB"}
    imgs[own_img:own_img + OWN, :] = unit_rows(img_ref[...])[0].astype(bf16)
    unit = unit_rows(txt_ref[...])[0].astype(bf16)
    txts[own_txt["A"]:own_txt["A"] + HALF, :] = unit[:HALF]
    txts[own_txt["B"]:own_txt["B"] + HALF, :] = unit[HALF:]
    line = img_ids_ref[...]
    img_ids[own_img // OWN] = jnp.concatenate([line] * 2, axis=1)
    line = txt_ids_ref[...]
    txt_ids[own_txt["A"] // HALF] = jnp.concatenate([line[:, :HALF]] * 4, axis=1)
    txt_ids[own_txt["B"] // HALF] = jnp.concatenate([line[:, HALF:]] * 4, axis=1)
    pl.semaphore_wait(barrier, len(near))

    first_axis, second_axis = {"A": "x", "B": "y"}, {"A": "y", "B": "x"}

    def text(path, second, first, low=0, high=HALF):
        row = txt_row(path, second, first)
        return txts.at[row + low:row + high, :]

    def text_id(path, second, first):
        return txt_ids.at[txt_row(path, second, first) // HALF]

    def image(dz, cr, low=0, high=OWN):
        row = IMG_ROW[dz, cr]
        return imgs.at[row + low:row + high, :]

    def image_id(dz, cr):
        return img_ids.at[IMG_ROW[dz, cr] // OWN]

    pieces = [(low, low + PIECE) for low in range(0, OWN, PIECE)]

    def send_text(p, src, dst, axis, way):
        send((p, *dst), text(p, *src), text(p, *dst), axis[p] + way)
        send((p, *dst, "id"), text_id(p, *src), text_id(p, *dst), axis[p] + way)

    def got_text(p, *slot):
        hop[(p, *slot)].wait_recv()
        hop[(p, *slot, "id")].wait_recv()

    def both_ways(e):
        for p in "AB":
            for d, way in ((1, "+"), (3, "-")):
                send_text(p, (0, e), (d, e), second_axis, way)

    def image_piece(dz, low, high):
        if dz:
            hop["z", dz, low].wait_recv()
        for src, way, step in ((dz, "+", 1), (dz, "-", -1)):
            dst = (dz + step) % 8
            if dz and (dz < 4) != (step > 0) or dz == 4:
                continue
            if dst == 4 and (low < HALF) != (step > 0):
                continue
            send(("z", dst, low), image(dz, 0, low, high), image(dst, 0, low, high), "z" + way)

    def image_ids(dz):
        if dz:
            hop["z", dz, "id"].wait_recv()
        for way, step in (("+", 1), ("-", -1)):
            dst = (dz + step) % 8
            if dz and (dz < 4) != (step > 0) or dz == 4 or dst == 4 and step < 0:
                continue
            send(("z", dst, "id"), image_id(dz, 0), image_id(dst, 0), "z" + way)

    def across(dz, low, high):
        send(("c", dz, low), image(dz, 0, low, high), image(dz, 1, low, high), "core")

    def across_ids(dz):
        send(("c", dz, "id"), image_id(dz, 0), image_id(dz, 1), "core")

    def pass_images(k, index):
        low, high = pieces[index]
        for dz in (k, 8 - k):
            image_piece(dz, low, high)
        if high == OWN:
            for dz in (k, 8 - k):
                image_ids(dz)
        for dz in (k, 8 - k):
            across(dz, low, high)
            if high == OWN:
                across_ids(dz)

    def got_images(*blocks):
        for dz in blocks:
            for low, _ in pieces:
                hop["c", dz, low].wait_recv()
            hop["c", dz, "id"].wait_recv()

    lane = lax.broadcasted_iota(jnp.int32, (1, 128), 1)

    def lines_of_text(*seconds):
        for d in seconds:
            for p in "AB":
                base, line = TXT_BASE[p, d], None
                for e in range(4):
                    ids = txt_ids[base // HALF + e]
                    line = ids if line is None else jnp.where(lane < HALF * e, line, ids)
                txt_line[:, base:base + 128] = line

    def columns_of_images(low, high):
        for row in range(low, high, 128):
            place = row // OWN
            line = jnp.where(lane < OWN, img_ids[place], img_ids[place + 1])
            img_col[row:row + 128, :] = jnp.transpose(jnp.broadcast_to(line, (128, 128)))

    scale = jnp.exp(jnp.full((1, 256), scale_ref[0], f32))
    half_scale, half_bias = 0.5 * scale, jnp.full((1, 256), 0.5 * bias_ref[0], f32)

    def score_tile(r, rows, t):
        scores = lax.dot_general(
            imgs[r:r + rows, :], txts[t:t + 256, :], (((1,), (1,)), ((), ())), preferred_element_type=f32
        )
        column = img_col[r:r + rows, :]
        same = jnp.concatenate([column, column], axis=1) == txt_line[:, t:t + 256]
        value = 0.5 * jnp.tanh(half_scale * scores + half_bias) + jnp.where(same, -0.5, 0.5)
        coef[r:r + rows, t:t + 256] = value.astype(bf16)

    for p in "AB":
        for e, way in ((1, "+"), (3, "-")):
            send_text(p, (0, 0), (0, e), first_axis, way)
    for low, high in pieces:
        image_piece(0, low, high)
    image_ids(0)
    both_ways(0)
    for low, high in pieces:
        across(0, low, high)
    across_ids(0)

    for p in "AB":
        got_text(p, 0, 1)
        got_text(p, 0, 3)
        send((p, 0, 2), text(p, 0, 1, 0, QUART), text(p, 0, 2, 0, QUART), first_axis[p] + "+")
        send((p, 0, 2, "id"), text_id(p, 0, 1), text_id(p, 0, 2), first_axis[p] + "+")
        send((p, 0, 2, "b"), text(p, 0, 3, QUART, HALF), text(p, 0, 2, QUART, HALF), first_axis[p] + "-")
        for d, way, order in ((1, "+", (1, 3)), (3, "-", (3, 1))):
            for e in order:
                send_text(p, (0, e), (d, e), second_axis, way)
    pass_images(1, 0)
    for p in "AB":
        got_text(p, 1, 0)
        send_text(p, (1, 0), (2, 0), second_axis, "+")
    pass_images(1, 1)
    for p in "AB":
        got_text(p, 3, 0)
        got_text(p, 0, 2)
        hop[p, 0, 2, "b"].wait_recv()
    both_ways(2)
    lines_of_text(0)
    pass_images(2, 0)
    got_images(0, 1, 7)
    columns_of_images(640, 1024)
    score_tile(640, 384, 768)
    for p in "AB":
        got_text(p, 1, 1)
        send_text(p, (1, 1), (2, 1), second_axis, "+")
        got_text(p, 3, 3)
        send_text(p, (3, 3), (2, 3), second_axis, "-")
    pass_images(2, 1)
    for p in "AB":
        got_text(p, 1, 3)
        got_text(p, 3, 1)
    got_images(2, 6)
    columns_of_images(384, 640)
    score_tile(384, 256, 768)
    pass_images(3, 0)
    for p in "AB":
        got_text(p, 1, 2)
        got_text(p, 3, 2)
        send_text(p, (3, 2), (2, 2), second_axis, "-")
    lines_of_text(1, 3)
    score_tile(384, 640, 256)
    pass_images(3, 1)
    score_tile(384, 640, 512)
    got_images(3, 5)
    columns_of_images(128, 384)
    score_tile(128, 256, 768)
    for low, high in pieces:
        image_piece(4, low, high)
        across(4, low, high)
    image_ids(4)
    across_ids(4)
    score_tile(128, 256, 256)
    score_tile(128, 256, 512)
    for p in "AB":
        for e in range(4):
            got_text(p, 2, e)
    lines_of_text(2)
    score_tile(128, 896, 0)
    got_images(4)
    columns_of_images(0, 128)
    for t in range(0, ROWS, 256):
        score_tile(0, 128, t)

    def img_terms(row, count):
        img_part[row:row + count, :] = jnp.dot(coef[row:row + count, :], txts[...], preferred_element_type=f32)

    def txt_terms(row, count):
        txt_part[row:row + count, :] = lax.dot_general(
            coef[:, row:row + count], imgs[...], (((0,), (0,)), ((), ())), preferred_element_type=f32
        )

    def to_core(*blocks):
        for dz in blocks:
            row, rows = IMG_ROW[dz, 1], slice(OWN * dz, OWN * dz + OWN)
            core_send[rows, :] = img_part[row:row + OWN, :].astype(bf16)
            send(("s", dz), core_send.at[rows], core_recv.at[rows], "core")

    def chip_sum(dz, low, high):
        row = IMG_ROW[dz, 0]
        return img_part[row + low:row + high, :] + core_recv[OWN * dz + low:OWN * dz + high, :].astype(f32)

    def z_far():
        hop["s", 4].wait_recv()
        for low, high in pieces:
            z_out(4, low, high, False, "-" if low < HALF else "+")

    def z_out(dz, low, high, before, way):
        rows = slice(OWN * dz + low, OWN * dz + high)
        total = chip_sum(dz, low, high)
        if before:
            hop["r", before, low].wait_recv()
            total = total + z_recv[OWN * before + low:OWN * before + high, :].astype(f32)
        z_send[rows, :] = total.astype(bf16)
        send(("r", dz, low), z_send.at[rows], z_recv.at[rows], "z" + way)

    def z_step(k, which):
        down, up = 4 - k, 4 + k
        for index in range(len(pieces) // 2):
            for dz, before, way, side in ((down, down + 1, "-", 1 - which), (up, up - 1, "+", which)):
                low, high = pieces[side * len(pieces) // 2 + index]
                z_out(dz, low, high, 0 if k == 1 and which == 0 else before, way)

    def txt_far():
        for e in (1, 2, 0, 3):
            for p in "AB":
                base, at = txt_row(p, 2, e), 128 * "AB".index(p) + HALF * e
                t1_send[at:at + HALF, :] = txt_part[base:base + HALF, :].astype(bf16)
                way = "-" if e < 2 else "+"
                send(("t1", p, e), t1_send.at[at:at + HALF], t1_recv.at[at:at + HALF], second_axis[p] + way)

    def txt_near(p, way, e):
        d = 1 if way == "-" else 3
        base, at = txt_row(p, d, e), 256 * "AB".index(p) + 128 * (d // 2) + HALF * e
        total = txt_part[base:base + HALF, :]
        if (way == "-") == (e < 2):
            got = 128 * "AB".index(p) + HALF * e
            hop["t1", p, e].wait_recv()
            total = total + t1_recv[got:got + HALF, :].astype(f32)
        t2_send[at:at + HALF, :] = total.astype(bf16)
        send(("t2", p, way, e), t2_send.at[at:at + HALF], t2_recv.at[at:at + HALF], second_axis[p] + way)

    def txt_line_sum(p, e):
        base, at = txt_row(p, 0, e), 256 * "AB".index(p) + HALF * e
        hop["t2", p, "-", e].wait_recv()
        hop["t2", p, "+", e].wait_recv()
        return (
            txt_part[base:base + HALF, :]
            + t2_recv[at:at + HALF, :].astype(f32)
            + t2_recv[at + 128:at + 128 + HALF, :].astype(f32)
        )

    def txt_far_first(p):
        at = HALF * "AB".index(p)
        t3_send[at:at + HALF, :] = txt_line_sum(p, 2).astype(bf16)
        for part, way in ((0, "-"), (1, "+")):
            rows = slice(at + QUART * part, at + QUART * part + QUART)
            send(("t3", p, part), t3_send.at[rows], t3_recv.at[rows], first_axis[p] + way)

    def txt_near_first(p, part):
        way, e = ("-", 1) if part == 0 else ("+", 3)
        total = txt_line_sum(p, e)
        at = OWN * "AB".index(p) + HALF * part
        for add in (0, 1):
            rows = slice(at + QUART * (part ^ 1 ^ add), at + QUART * (part ^ 1 ^ add) + QUART)
            piece = total[QUART * (part ^ 1 ^ add):QUART * (part ^ 1 ^ add) + QUART]
            if add:
                hop["t3", p, part].wait_recv()
                got = HALF * "AB".index(p) + QUART * part
                piece = piece + t3_recv[got:got + QUART, :].astype(f32)
            t4_send[rows, :] = piece.astype(bf16)
            send(("t4", p, part, add), t4_send.at[rows], t4_recv.at[rows], first_axis[p] + way)

    def finish(embedding, total):
        unit, inverse = unit_rows(embedding)
        direction = scale[:, 0:1] * total
        return inverse * (direction - unit * jnp.sum(unit * direction, axis=1, keepdims=True))

    img_terms(0, 128)
    to_core(4)
    txt_terms(0, 256)
    txt_far()
    img_terms(128, 256)
    to_core(3, 5)
    z_far()
    txt_terms(256, 256)
    txt_near("A", "-", 2)
    txt_near("A", "+", 1)
    txt_near("A", "-", 3)
    txt_terms(512, 256)
    txt_near("B", "-", 2)
    txt_near("B", "+", 1)
    txt_near("B", "-", 3)
    hop["s", 3].wait_recv()
    hop["s", 5].wait_recv()
    z_step(1, 0)
    img_terms(384, 256)
    to_core(2, 6)
    for p in "AB":
        txt_near(p, "+", 2)
        txt_near(p, "-", 1)
    z_step(1, 1)
    img_terms(640, 384)
    to_core(1, 7, 0)
    hop["s", 2].wait_recv()
    hop["s", 6].wait_recv()
    z_step(2, 0)
    for p in "AB":
        txt_near(p, "+", 3)
        txt_near(p, "-", 0)
        txt_near(p, "+", 0)
    txt_terms(768, 256)
    z_step(2, 1)
    txt_far_first("A")
    txt_far_first("B")
    hop["s", 1].wait_recv()
    hop["s", 7].wait_recv()
    z_step(3, 0)
    for p in "AB":
        for part in (0, 1):
            txt_near_first(p, part)
    z_step(3, 1)
    for p in "AB":
        low = HALF * "AB".index(p)
        total = txt_line_sum(p, 0)
        for part in (0, 1):
            for add in (0, 1):
                hop["t4", p, part, add].wait_recv()
            at = OWN * "AB".index(p) + HALF * part
            total = total + t4_recv[at:at + HALF, :].astype(f32)
        txt_out[low:low + HALF, :] = finish(txt_ref[low:low + HALF, :], total)
    hop["s", 0].wait_recv()
    for side in (1, 0):
        low, high = HALF * side, HALF * side + HALF
        total = chip_sum(0, low, high)
        for dz in (1, 7):
            for a, b in pieces:
                if low <= a and b <= high:
                    hop["r", dz, a].wait_recv()
            total = total + z_recv[OWN * dz + low:OWN * dz + high, :].astype(f32)
        img_out[low:high, :] = finish(img_ref[low:high, :], total)
    for copy in started:
        copy.wait_send()


def body(img_emb, txt_emb, img_ids, txt_ids, scale_logarithm, bias):
    f32, bf16, i32 = jnp.float32, jnp.bfloat16, jnp.int32
    vmem, smem = pl.BlockSpec(memory_space=pltpu.VMEM), pl.BlockSpec(memory_space=pltpu.SMEM)
    return pl.pallas_call(
        kernel,
        out_shape=(jax.ShapeDtypeStruct((OWN, D), f32), jax.ShapeDtypeStruct((OWN, D), f32)),
        in_specs=[vmem, vmem, vmem, vmem, smem, smem],
        out_specs=(vmem, vmem),
        scratch_shapes=[
            pltpu.VMEM((ROWS, D), bf16),
            pltpu.VMEM((ROWS, D), bf16),
            pltpu.VMEM((16, 1, 128), i32),
            pltpu.VMEM((32, 1, 128), i32),
            pltpu.VMEM((ROWS, 128), i32),
            pltpu.VMEM((1, ROWS), i32),
            pltpu.VMEM((ROWS, ROWS), bf16),
            pltpu.VMEM((ROWS, D), f32),
            pltpu.VMEM((ROWS, D), f32),
            pltpu.VMEM((256, D), bf16),
            pltpu.VMEM((256, D), bf16),
            pltpu.VMEM((512, D), bf16),
            pltpu.VMEM((512, D), bf16),
            pltpu.VMEM((64, D), bf16),
            pltpu.VMEM((64, D), bf16),
            pltpu.VMEM((128, D), bf16),
            pltpu.VMEM((128, D), bf16),
            pltpu.VMEM((512, D), bf16),
            pltpu.VMEM((512, D), bf16),
            pltpu.VMEM((512, D), bf16),
            pltpu.VMEM((512, D), bf16),
            pltpu.SemaphoreType.DMA((N_COPIES,)),
            pltpu.SemaphoreType.DMA((N_COPIES,)),
        ],
        compiler_params=pltpu.CompilerParams(
            collective_id=0, has_side_effects=True, vmem_limit_bytes=56 * 1024 * 1024
        ),
        cost_estimate=pl.CostEstimate(flops=7247757312, bytes_accessed=900000, transcendentals=1048576),
    )(img_emb, txt_emb, img_ids.reshape(1, OWN), txt_ids.reshape(1, OWN), scale_logarithm, bias)


def solution(mesh):
    split = P(("blk", "group"), None)
    ids = P(("blk", "group"))
    return jax.shard_map(
        body,
        mesh=mesh,
        in_specs=(split, split, ids, ids, P(), P()),
        out_specs=(split, split),
        check_vma=False,
    )
```

```python
import functools

import jax
import jax.numpy as jnp
from jax import lax
from jax.experimental import pallas as pl
from jax.experimental.pallas import tpu as pltpu
from jax.sharding import PartitionSpec as P

MESH = pl.DeviceIdType.MESH
D = 1152
OWN = 64
HALF = 32
QUART = 16
ROWS = 1024
PIECE = 16
N_ARRIVALS = 134
N_SENT = 6

LINK_ROW, CORE_ROW, LINK_WAIT, CORE_WAIT, ISSUE, QUEUE = 0.0493, 0.0035, 2.0, 1.7, 0.03, 1.6

IMG_ORDER = [
    (4, 1), (4, 0),
    (3, 1), (5, 1), (3, 0), (5, 0),
    (2, 1), (6, 1), (2, 0), (6, 0),
    (1, 1), (7, 1), (0, 1), (1, 0), (7, 0), (0, 0),
]
IMG_ROW = {key: OWN * place for place, key in enumerate(IMG_ORDER)}

TXT_BASE = {
    ("A", 2): 0, ("B", 2): 128,
    ("A", 1): 256, ("A", 3): 384, ("B", 1): 512, ("B", 3): 640,
    ("A", 0): 768, ("B", 0): 896,
}


def txt_row(path, second, first):
    return TXT_BASE[path, second] + HALF * first


def unit_rows(embedding):
    widened = embedding.astype(jnp.float32)
    inverse = lax.rsqrt(jnp.sum(widened * widened, axis=1, keepdims=True) + 1e-06)
    return widened * inverse, inverse


class Plan:
    def __init__(self):
        self.steps, self.group_of, self.groups = {}, {}, {}

    def work(self, key, needs, cost, run):
        self.steps[key] = (tuple(needs), cost, run, None, 0.0)

    def copy(self, key, needs, rows, src, dst, to, group=None):
        length = rows * (CORE_ROW if to == "core" else LINK_ROW)
        self.steps[key] = (tuple(needs), length, (src, dst, to), to, CORE_WAIT if to == "core" else LINK_WAIT)
        self.group_of[key] = group or key
        self.groups.setdefault(group or key, []).append(key)

    def all_needs(self, key):
        result = []
        for need in self.steps[key][0]:
            result += self.groups[self.group_of[need]] if need in self.group_of else [need]
        return tuple(dict.fromkeys(result))

    def order(self):
        steps = {key: (self.all_needs(key), *step[1:]) for key, step in self.steps.items()}
        users = {key: [] for key in steps}
        for key, step in steps.items():
            for need in step[0]:
                users[need].append(key)
        left = {}

        def to_end(key):
            if key not in left:
                left[key] = steps[key][1] + steps[key][4] + max([to_end(user) for user in users[key]], default=0.0)
            return left[key]

        rank = {key: (-to_end(key), number) for number, key in enumerate(steps)}
        now, ready, free, end, result = 0.0, {}, {}, {}, []
        missing = {key: len(step[0]) for key, step in steps.items()}
        for key in steps:
            if not missing[key]:
                ready[key] = 0.0
        while ready:
            def opens(key):
                link = steps[key][3]
                return ready[key] if link is None else max(ready[key], free.get(link, 0.0) - QUEUE)

            now = max(now, min(opens(key) for key in ready))
            able = [key for key in ready if opens(key) <= now]
            key = min(able, key=lambda key: (steps[key][3] is None, rank[key]))
            del ready[key]
            needs, length, run, link, wait = steps[key]
            if link is None:
                now += length
                end[key] = now
            else:
                now += ISSUE
                free[link] = max(now, free.get(link, 0.0)) + length
                end[key] = free[link] + wait
            result.append(key)
            for user in users[key]:
                missing[user] -= 1
                if not missing[user]:
                    ready[user] = max(end[need] for need in steps[user][0])
        return result, end


def kernel(
    img_in, txt_in, img_ids_in, txt_ids_in, scale_in, bias_in, img_out, txt_out,
    img_ref, txt_ref, img_ids_ref, txt_ids_ref, scale_ref, bias_ref, in_sems,
    imgs, txts, img_ids, txt_ids, img_col, txt_line, coef, img_part, txt_part,
    t1_send, t1_recv, t2_send, t2_recv, t3_send, t3_recv, t4_send, t4_recv,
    core_send, core_recv, z_send, z_recv, send_sems, recv_sems,
):
    f32, bf16 = jnp.float32, jnp.bfloat16
    blk, grp = lax.axis_index("blk"), lax.axis_index("group")
    y, x_hi = lax.div(blk, 2), lax.rem(blk, 2)
    z, x_lo, core = lax.div(grp, 4), lax.rem(lax.div(grp, 2), 2), lax.rem(grp, 2)
    x = x_hi * 2 + x_lo

    def device(dx=0, dy=0, dz=0, dc=0):
        nx, ny, nz = lax.rem(x + dx + 4, 4), lax.rem(y + dy + 4, 4), lax.rem(z + dz + 8, 8)
        nc = lax.rem(core + dc, 2)
        return (ny * 2 + lax.div(nx, 2), (nz * 2 + lax.rem(nx, 2)) * 2 + nc)

    near = {
        "x+": device(dx=1), "x-": device(dx=-1), "y+": device(dy=1), "y-": device(dy=-1),
        "z+": device(dz=1), "z-": device(dz=-1), "core": device(dc=1),
    }
    barrier = pltpu.get_barrier_semaphore()
    for there in near.values():
        pl.semaphore_signal(barrier, inc=1, device_id=there, device_id_type=MESH)

    loads = [
        pltpu.make_async_copy(src, dst, in_sems.at[number])
        for number, (src, dst) in enumerate([
            (img_in, img_ref), (txt_in, txt_ref), (img_ids_in, img_ids_ref), (txt_ids_in, txt_ids_ref),
            (scale_in, scale_ref), (bias_in, bias_ref),
        ])
    ]
    for load in loads:
        load.start()
    for load in loads:
        load.wait()
    own_img, own_txt = IMG_ROW[0, 0], {p: txt_row(p, 0, 0) for p in "AB"}
    imgs[own_img:own_img + OWN, :] = unit_rows(img_ref[...])[0].astype(bf16)
    unit = unit_rows(txt_ref[...])[0].astype(bf16)
    txts[own_txt["A"]:own_txt["A"] + HALF, :] = unit[:HALF]
    txts[own_txt["B"]:own_txt["B"] + HALF, :] = unit[HALF:]
    line = img_ids_ref[...]
    img_ids[own_img // OWN] = jnp.concatenate([line] * 2, axis=1)
    line = txt_ids_ref[...]
    txt_ids[own_txt["A"] // HALF] = jnp.concatenate([line[:, :HALF]] * 4, axis=1)
    txt_ids[own_txt["B"] // HALF] = jnp.concatenate([line[:, HALF:]] * 4, axis=1)
    scale = jnp.exp(jnp.broadcast_to(scale_ref[...], (1, 256)))
    half_scale, half_bias = 0.5 * scale, 0.5 * jnp.broadcast_to(bias_ref[...], (1, 256))
    pl.semaphore_wait(barrier, len(near))

    plan = Plan()
    first_axis, second_axis = {"A": "x", "B": "y"}, {"A": "y", "B": "x"}
    halves = (0, 1)

    def move_text(p, src, dst, piece, to, needs):
        low = piece * QUART
        a, b = txt_row(p, *src) + low, txt_row(p, *dst) + low
        d, e = dst
        group = ("t", p, d) if d == 2 or (d == 1 and e > 1) or (d == 3 and e < 2) else None
        plan.copy(("t", p, *dst, piece), needs, QUART, txts.at[a:a + QUART, :], txts.at[b:b + QUART, :], to, group)

    def move_text_ids(p, src, dst, count, to, needs):
        a, b = txt_row(p, *src) // HALF, txt_row(p, *dst) // HALF
        group = ("ti", p, dst[0]) if dst in ((0, 2), (0, 3), (2, 0), (2, 2)) else None
        plan.copy(("ti", p, *dst), needs, 1, txt_ids.at[a:a + count], txt_ids.at[b:b + count], to, group)

    def text_here(p, d, e, piece):
        return [] if (d, e) == (0, 0) else [("t", p, d, e, piece)]

    for p in "AB":
        one, two = first_axis[p], second_axis[p]
        for e, way, order in ((1, "+", (0, 1)), (3, "-", (1, 0))):
            for piece in order:
                move_text(p, (0, 0), (0, e), piece, one + way, [])
        move_text(p, (0, 1), (0, 2), 0, one + "+", [("t", p, 0, 1, 0)])
        move_text(p, (0, 3), (0, 2), 1, one + "-", [("t", p, 0, 3, 1)])
        for e in range(4):
            for piece in halves:
                for d, way in ((1, "+"), (3, "-")):
                    move_text(p, (0, e), (d, e), piece, two + way, text_here(p, 0, e, piece))
                d, way = (1, "+") if e < 2 else (3, "-")
                move_text(p, (d, e), (2, e), piece, two + way, [("t", p, d, e, piece)])
        move_text_ids(p, (0, 0), (0, 1), 1, one + "+", [])
        move_text_ids(p, (0, 0), (0, 3), 1, one + "-", [])
        move_text_ids(p, (0, 1), (0, 2), 1, one + "+", [("ti", p, 0, 1)])
        line_ids = [("ti", p, 0, e) for e in (1, 2, 3)]
        move_text_ids(p, (0, 0), (1, 0), 4, two + "+", line_ids)
        move_text_ids(p, (0, 0), (3, 0), 4, two + "-", line_ids)
        move_text_ids(p, (1, 0), (2, 0), 2, two + "+", [("ti", p, 1, 0)])
        move_text_ids(p, (3, 2), (2, 2), 2, two + "-", [("ti", p, 3, 0)])

    pieces = [(low, low + PIECE) for low in range(0, OWN, PIECE)]

    def move_image(src, dst, low, high, to, needs):
        a, b = IMG_ROW[src, 0], IMG_ROW[dst, 0]
        group = ("z", 4, "half", low // HALF) if dst == 4 else None
        plan.copy(
            ("z", dst, low), needs, high - low, imgs.at[a + low:a + high, :], imgs.at[b + low:b + high, :], to, group
        )

    for way, step in (("+", 1), ("-", -1)):
        for hops in range(1, 5):
            src, dst = (hops - 1) * step % 8, hops * step % 8
            for low, high in pieces[::step]:
                if hops < 4 or (low < HALF) == (step > 0):
                    move_image(src, dst, low, high, "z" + way, [("z", src, low)] if src else [])
            if hops < 4 or step > 0:
                plan.copy(
                    ("zi", dst), [("zi", src)] if src else [], 1,
                    img_ids.at[IMG_ROW[src, 0] // OWN], img_ids.at[IMG_ROW[dst, 0] // OWN], "z" + way,
                )
    for dz in range(8):
        a, b = IMG_ROW[dz, 0], IMG_ROW[dz, 1]
        pair = min(dz, 8 - dz) or 1
        for half in halves:
            low, high = half * HALF, half * HALF + HALF
            plan.copy(
                ("c", dz, half), [("z", dz, at) for at, _ in pieces if low <= at < high and dz], HALF,
                imgs.at[a + low:a + high, :], imgs.at[b + low:b + high, :], "core", ("c", pair),
            )
        plan.copy(
            ("ci", dz), [("zi", dz)] if dz else [], 1, img_ids.at[a // OWN], img_ids.at[b // OWN], "core",
            ("ci", pair),
        )

    lane = lax.broadcasted_iota(jnp.int32, (1, 128), 1)

    def line_of_text(base):
        line = None
        for e in range(4):
            ids = txt_ids[base // HALF + e]
            line = ids if line is None else jnp.where(lane < HALF * e, line, ids)
        txt_line[:, base:base + 128] = line

    for (p, d), base in TXT_BASE.items():
        ids = {0: [("ti", p, 0, e) for e in (1, 2, 3)], 2: [("ti", p, 2, 0), ("ti", p, 2, 2)]}.get(d, [("ti", p, d, 0)])
        plan.work(("line", base), ids, 0.05, functools.partial(line_of_text, base))

    def column_of_images(row):
        place = row // OWN
        line = jnp.where(lane < OWN, img_ids[place], img_ids[place + 1])
        img_col[row:row + 128, :] = jnp.transpose(jnp.broadcast_to(line, (128, 128)))

    for row in range(0, ROWS, 128):
        ids = []
        for dz, cr in IMG_ORDER[row // OWN:row // OWN + 2]:
            ids += [("ci", dz)] if cr else [("zi", dz)] if dz else []
        plan.work(("column", row), ids, 0.1, functools.partial(column_of_images, row))

    def score_tile(r, rows, t):
        scores = lax.dot_general(
            imgs[r:r + rows, :], txts[t:t + 256, :], (((1,), (1,)), ((), ())), preferred_element_type=f32
        )
        column = img_col[r:r + rows, :]
        same = jnp.concatenate([column, column], axis=1) == txt_line[:, t:t + 256]
        value = 0.5 * jnp.tanh(half_scale * scores + half_bias) + jnp.where(same, -0.5, 0.5)
        coef[r:r + rows, t:t + 256] = value.astype(bf16)

    score_keys = []
    for t, cuts in ((768, (640, 384, 128, 0)), (256, (384, 128, 0)), (512, (384, 128, 0)), (0, (128, 0))):
        high = ROWS
        for r in cuts:
            needs = [("column", row) for row in range(r, high, 128)] + [("line", t), ("line", t + 128)]
            for dz, cr in IMG_ORDER[r // OWN:high // OWN]:
                needs += [("c", dz, half) for half in halves] if cr else [("z", dz, at) for at, _ in pieces if dz]
            for (p, d), base in TXT_BASE.items():
                if t <= base < t + 256:
                    needs += [at for e in range(4) for piece in halves for at in text_here(p, d, e, piece)]
            key = ("score", r, high, t)
            score_keys.append(key)
            plan.work(key, needs, 0.25 + 0.00056 * (high - r), functools.partial(score_tile, r, high - r, t))
            high = r

    def img_terms(row):
        img_part[row:row + 128, :] = jnp.dot(coef[row:row + 128, :], txts[...], preferred_element_type=f32)

    def txt_terms(row):
        txt_part[row:row + 128, :] = lax.dot_general(
            coef[:, row:row + 128], imgs[...], (((0,), (0,)), ((), ())), preferred_element_type=f32
        )

    for row in range(0, ROWS, 128):
        needs = [key for key in score_keys if key[1] <= row < key[2]]
        plan.work(("img", row), needs, 0.37, functools.partial(img_terms, row))
        needs = [key for key in score_keys if key[3] <= row < key[3] + 256]
        plan.work(("txt", row), needs, 0.38, functools.partial(txt_terms, row))

    def img_key(dz, cr):
        return ("img", IMG_ROW[dz, cr] // 128 * 128)

    def to_core(dz):
        row = IMG_ROW[dz, 1]
        core_send[OWN * dz:OWN * dz + OWN, :] = img_part[row:row + OWN, :].astype(bf16)

    def chip_sum(dz, low, high):
        row = IMG_ROW[dz, 0]
        return img_part[row + low:row + high, :] + core_recv[OWN * dz + low:OWN * dz + high, :].astype(f32)

    def z_out(dz, low, high, before):
        total = chip_sum(dz, low, high)
        if before:
            total = total + z_recv[OWN * before + low:OWN * before + high, :].astype(f32)
        z_send[OWN * dz + low:OWN * dz + high, :] = total.astype(bf16)

    for dz in range(8):
        rows = slice(OWN * dz, OWN * dz + OWN)
        plan.work(("to core", dz), [img_key(dz, 1)], 0.12, functools.partial(to_core, dz))
        plan.copy(("s", dz), [("to core", dz)], OWN, core_send.at[rows], core_recv.at[rows], "core", ("s", min(dz, 8 - dz)))
    for dz in (4, 3, 5, 2, 6, 1, 7):
        for low, high in pieces:
            if dz == 4:
                way, before = ("-" if low < HALF else "+"), 0
            else:
                way, before = ("-", dz + 1) if dz < 4 else ("+", dz - 1)
                if before == 4 and (low < HALF) != (way == "-"):
                    before = 0
            needs = [img_key(dz, 0), ("s", dz)] + ([("r", before, low)] if before else [])
            plan.work(("z out", dz, low), needs, 0.08, functools.partial(z_out, dz, low, high, before))
            rows = slice(OWN * dz + low, OWN * dz + high)
            plan.copy(
                ("r", dz, low), [("z out", dz, low)], high - low, z_send.at[rows], z_recv.at[rows], "z" + way,
                ("r", 1, "half", low // HALF) if dz in (1, 7) else None,
            )

    def t1_out(p, e):
        base, at = txt_row(p, 2, e), 128 * "AB".index(p) + HALF * e
        t1_send[at:at + HALF, :] = txt_part[base:base + HALF, :].astype(bf16)

    def t2_out(p, d, e, added):
        base, at = txt_row(p, d, e), 256 * "AB".index(p) + 128 * (d // 2) + HALF * e
        total = txt_part[base:base + HALF, :]
        if added:
            got = 128 * "AB".index(p) + HALF * e
            total = total + t1_recv[got:got + HALF, :].astype(f32)
        t2_send[at:at + HALF, :] = total.astype(bf16)

    def line_sum(p, e, low=0, high=HALF):
        base, at = txt_row(p, 0, e), 256 * "AB".index(p) + HALF * e
        return (
            txt_part[base + low:base + high, :]
            + t2_recv[at + low:at + high, :].astype(f32)
            + t2_recv[at + 128 + low:at + 128 + high, :].astype(f32)
        )

    def t3_out(p, part):
        at = HALF * "AB".index(p) + QUART * part
        t3_send[at:at + QUART, :] = line_sum(p, 2, QUART * part, QUART * part + QUART).astype(bf16)

    def t4_out(p, side, part):
        at = OWN * "AB".index(p) + HALF * side + QUART * part
        total = line_sum(p, 1 + 2 * side, QUART * part, QUART * part + QUART)
        if part == side:
            got = HALF * "AB".index(p) + QUART * part
            total = total + t3_recv[got:got + QUART, :].astype(f32)
        t4_send[at:at + QUART, :] = total.astype(bf16)

    def line_needs(p, e):
        return [("txt", TXT_BASE[p, 0]), ("t2", p, 1, e), ("t2", p, 3, e)]

    for p in "AB":
        one, two = first_axis[p], second_axis[p]
        for e in range(4):
            at = 128 * "AB".index(p) + HALF * e
            plan.work(("t1 out", p, e), [("txt", TXT_BASE[p, 2])], 0.1, functools.partial(t1_out, p, e))
            plan.copy(
                ("t1", p, e), [("t1 out", p, e)], HALF, t1_send.at[at:at + HALF], t1_recv.at[at:at + HALF],
                two + ("-" if e < 2 else "+"),
            )
            for d, way in ((1, "-"), (3, "+")):
                added = (d == 1) == (e < 2)
                at = 256 * "AB".index(p) + 128 * (d // 2) + HALF * e
                needs = [("txt", TXT_BASE[p, d])] + ([("t1", p, e)] if added else [])
                plan.work(("t2 out", p, d, e), needs, 0.12, functools.partial(t2_out, p, d, e, added))
                plan.copy(
                    ("t2", p, d, e), [("t2 out", p, d, e)], HALF, t2_send.at[at:at + HALF], t2_recv.at[at:at + HALF],
                    two + way, ("t2", p, e),
                )
        for part, way in ((0, "-"), (1, "+")):
            at = HALF * "AB".index(p) + QUART * part
            plan.work(("t3 out", p, part), line_needs(p, 2), 0.08, functools.partial(t3_out, p, part))
            plan.copy(
                ("t3", p, part), [("t3 out", p, part)], QUART, t3_send.at[at:at + QUART], t3_recv.at[at:at + QUART],
                one + way,
            )
        for side, way in ((0, "-"), (1, "+")):
            for part in halves:
                at = OWN * "AB".index(p) + HALF * side + QUART * part
                needs = line_needs(p, 1 + 2 * side) + ([("t3", p, part)] if part == side else [])
                plan.work(("t4 out", p, side, part), needs, 0.08, functools.partial(t4_out, p, side, part))
                plan.copy(
                    ("t4", p, side, part), [("t4 out", p, side, part)], QUART,
                    t4_send.at[at:at + QUART], t4_recv.at[at:at + QUART], one + way, ("t4", p),
                )

    def finish(embedding, total):
        unit, inverse = unit_rows(embedding)
        direction = scale[:, 0:1] * total
        return inverse * (direction - unit * jnp.sum(unit * direction, axis=1, keepdims=True))

    def finish_txt(p):
        low = HALF * "AB".index(p)
        total = line_sum(p, 0)
        for side in halves:
            at = OWN * "AB".index(p) + HALF * side
            total = total + t4_recv[at:at + HALF, :].astype(f32)
        txt_out[low:low + HALF, :] = finish(txt_ref[low:low + HALF, :], total)

    def finish_img(low, high):
        total = chip_sum(0, low, high)
        for dz in (1, 7):
            total = total + z_recv[OWN * dz + low:OWN * dz + high, :].astype(f32)
        img_out[low:high, :] = finish(img_ref[low:high, :], total)

    for p in "AB":
        needs = line_needs(p, 0) + [("t4", p, side, part) for side in halves for part in halves]
        plan.work(("end", p), needs, 0.2, functools.partial(finish_txt, p))
    for low in (HALF, 0):
        needs = [img_key(0, 0), ("s", 0), ("r", 1, low)]
        plan.work(("end", low), needs, 0.15, functools.partial(finish_img, low, low + HALF))

    arrives = {group: recv_sems.at[number] for number, group in enumerate(plan.groups)}
    sent = []

    def whole(rows, ids):
        return txt_ids.at[0:rows] if ids else imgs.at[0:rows, :]

    def await_copy(ref, sem):
        pltpu.make_async_copy(ref, ref, sem).wait()

    here = set()
    for key in plan.order()[0]:
        needs, _, run, link, _ = plan.steps[key]
        for need in needs:
            group = plan.group_of.get(need)
            if group is None or group in here:
                continue
            here.add(group)
            landed = [plan.steps[member][2][1] for member in plan.groups[group]]
            ids = landed[0].dtype != bf16
            await_copy(whole(sum(1 if ref.ndim == 2 and ids else ref.shape[0] for ref in landed), ids), arrives[group])
        if link is None:
            run()
            continue
        src, dst, to = run
        ids = src.dtype != bf16
        rows = 1 if src.ndim == 2 and ids else src.shape[0]
        open_sems = [entry for entry in sent if entry[0] == ids and entry[1] + rows <= (32 if ids else ROWS)]
        if not open_sems:
            open_sems = [[ids, 0, send_sems.at[len(sent)]]]
            sent.append(open_sems[0])
        open_sems[0][1] += rows
        pltpu.make_async_remote_copy(
            src_ref=src, dst_ref=dst, send_sem=open_sems[0][2], recv_sem=arrives[plan.group_of[key]],
            device_id=near[to], device_id_type=MESH,
        ).start()
    for ids, rows, sem in sent:
        await_copy(whole(rows, ids), sem)


def write_out(img_grad, txt_grad, img_out, txt_out, sems):
    copies = [
        pltpu.make_async_copy(src, dst, sems.at[number])
        for number, (src, dst) in enumerate([(img_grad, img_out), (txt_grad, txt_out)])
    ]
    for copy in copies:
        copy.start()
    for copy in copies:
        copy.wait()


def body(img_emb, txt_emb, img_ids, txt_ids, scale_logarithm, bias):
    f32, bf16, i32 = jnp.float32, jnp.bfloat16, jnp.int32
    anywhere = pl.BlockSpec(memory_space=pl.ANY)
    in_vmem = pl.BlockSpec(memory_space=pltpu.VMEM)
    grads = pl.pallas_call(
        kernel,
        out_shape=(pltpu.VMEM((OWN, D), f32), pltpu.VMEM((OWN, D), f32)),
        in_specs=[anywhere] * 6,
        out_specs=(in_vmem, in_vmem),
        scratch_shapes=[
            pltpu.VMEM((OWN, D), bf16),
            pltpu.VMEM((OWN, D), bf16),
            pltpu.VMEM((1, OWN), i32),
            pltpu.VMEM((1, OWN), i32),
            pltpu.VMEM((1, 1), f32),
            pltpu.VMEM((1, 1), f32),
            pltpu.SemaphoreType.DMA((6,)),
            pltpu.VMEM((ROWS, D), bf16),
            pltpu.VMEM((ROWS, D), bf16),
            pltpu.VMEM((16, 1, 128), i32),
            pltpu.VMEM((32, 1, 128), i32),
            pltpu.VMEM((ROWS, 128), i32),
            pltpu.VMEM((1, ROWS), i32),
            pltpu.VMEM((ROWS, ROWS), bf16),
            pltpu.VMEM((ROWS, D), f32),
            pltpu.VMEM((ROWS, D), f32),
            pltpu.VMEM((256, D), bf16),
            pltpu.VMEM((256, D), bf16),
            pltpu.VMEM((512, D), bf16),
            pltpu.VMEM((512, D), bf16),
            pltpu.VMEM((64, D), bf16),
            pltpu.VMEM((64, D), bf16),
            pltpu.VMEM((128, D), bf16),
            pltpu.VMEM((128, D), bf16),
            pltpu.VMEM((512, D), bf16),
            pltpu.VMEM((512, D), bf16),
            pltpu.VMEM((512, D), bf16),
            pltpu.VMEM((512, D), bf16),
            pltpu.SemaphoreType.DMA((N_SENT,)),
            pltpu.SemaphoreType.DMA((N_ARRIVALS,)),
        ],
        compiler_params=pltpu.CompilerParams(
            collective_id=0, has_side_effects=True, vmem_limit_bytes=56 * 1024 * 1024
        ),
        cost_estimate=pl.CostEstimate(flops=7247757312, bytes_accessed=900000, transcendentals=1048576),
    )(img_emb, txt_emb, img_ids.reshape(1, OWN), txt_ids.reshape(1, OWN),
      scale_logarithm.reshape(1, 1), bias.reshape(1, 1))
    return pl.pallas_call(
        write_out,
        out_shape=(jax.ShapeDtypeStruct((OWN, D), f32), jax.ShapeDtypeStruct((OWN, D), f32)),
        in_specs=[in_vmem, in_vmem],
        out_specs=(anywhere, anywhere),
        scratch_shapes=[pltpu.SemaphoreType.DMA((2,))],
    )(*[pltpu.with_memory_space_constraint(grad, pltpu.VMEM) for grad in grads])


def solution(mesh):
    split = P(("blk", "group"), None)
    ids = P(("blk", "group"))
    return jax.shard_map(
        body,
        mesh=mesh,
        in_specs=(split, split, ids, ids, P(), P()),
        out_specs=(split, split),
        check_vma=False,
    )
```

```python
import functools

import jax
import jax.numpy as jnp
from jax import lax
from jax.experimental import pallas as pl
from jax.experimental.pallas import tpu as pltpu
from jax.sharding import PartitionSpec as P

MESH = pl.DeviceIdType.MESH
D = 1152
OWN = 64
HALF = 32
QUART = 16
ROWS = 1024
PIECE = 16
N_ARRIVALS = 146
N_SENT = 6

LINK_ROW, CORE_ROW, LINK_WAIT, CORE_WAIT, ISSUE, QUEUE = 0.0493, 0.0035, 2.2, 1.7, 0.03, 1.6
ROUTE = {
    **{way: ((way,), 1, 0.0) for way in ("x+", "x-", "y+", "y-", "z+", "z-", "core")},
    "x2": (("x+", "x-"), 1, 0.6), "y2": (("y+", "y-"), 1, 0.6), "z+2": (("z+",), 2, 0.6), "z-2": (("z-",), 2, 0.6),
}

IMG_ORDER = [
    (4, 1), (4, 0),
    (3, 1), (5, 1), (3, 0), (5, 0),
    (2, 1), (6, 1), (2, 0), (6, 0),
    (1, 1), (7, 1), (0, 1), (1, 0), (7, 0), (0, 0),
]
IMG_ROW = {key: OWN * place for place, key in enumerate(IMG_ORDER)}

TXT_ORDER = (
    [(p, 2, e) for p in "AB" for e in range(4)]
    + [(p, d, e) for p in "AB" for d, e in ((1, 2), (1, 3), (3, 0), (3, 1))]
    + [(p, d, e) for p in "AB" for d, e in ((1, 0), (1, 1), (3, 2), (3, 3))]
    + [(p, 0, e) for p in "AB" for e in range(4)]
)
TXT_ROW = {key: HALF * place for place, key in enumerate(TXT_ORDER)}


SCORE_TILES = [
    (640, 1024, 768, 1024), (384, 640, 768, 1024), (128, 384, 768, 1024),
    (384, 1024, 512, 768), (128, 384, 512, 768),
    (384, 1024, 256, 512), (128, 384, 256, 512),
    (128, 1024, 0, 256),
    (0, 128, 0, 1024),
]


def unit_rows(embedding):
    widened = embedding.astype(jnp.float32)
    inverse = lax.rsqrt(jnp.sum(widened * widened, axis=1, keepdims=True) + 1e-06)
    return widened * inverse, inverse


class Plan:
    def __init__(self):
        self.steps, self.group_of, self.groups = {}, {}, {}

    def work(self, key, needs, cost, run):
        self.steps[key] = (tuple(needs), cost, run, None, 0.0)

    def copy(self, key, needs, rows, src, dst, to, group=None):
        links, times, more = ROUTE[to]
        length = rows * times * (CORE_ROW if to == "core" else LINK_ROW)
        wait = CORE_WAIT if to == "core" else LINK_WAIT + more
        self.steps[key] = (tuple(needs), length, (src, dst, to), links, wait)
        self.group_of[key] = group or key
        self.groups.setdefault(group or key, []).append(key)

    def all_needs(self, key):
        result = []
        for need in self.steps[key][0]:
            result += self.groups[self.group_of[need]] if need in self.group_of else [need]
        return tuple(dict.fromkeys(result))

    def order(self):
        steps = {key: (self.all_needs(key), *step[1:]) for key, step in self.steps.items()}
        users = {key: [] for key in steps}
        for key, step in steps.items():
            for need in step[0]:
                users[need].append(key)
        left = {}

        def to_end(key):
            if key not in left:
                left[key] = steps[key][1] + steps[key][4] + max([to_end(user) for user in users[key]], default=0.0)
            return left[key]

        rank = {key: (-to_end(key), number) for number, key in enumerate(steps)}
        now, ready, free, end, result = 0.0, {}, {}, {}, []
        missing = {key: len(step[0]) for key, step in steps.items()}
        for key in steps:
            if not missing[key]:
                ready[key] = 0.0
        while ready:
            def opens(key):
                links = steps[key][3] or ()
                return max([ready[key]] + [free.get(link, 0.0) - QUEUE for link in links])

            now = max(now, min(opens(key) for key in ready))
            able = [key for key in ready if opens(key) <= now]
            key = min(able, key=lambda key: (steps[key][3] is None, rank[key]))
            del ready[key]
            needs, length, run, links, wait = steps[key]
            if links is None:
                now += length
                end[key] = now
            else:
                now += ISSUE
                for link in links:
                    free[link] = max(now, free.get(link, 0.0)) + length
                end[key] = max(free[link] for link in links) + wait
            result.append(key)
            for user in users[key]:
                missing[user] -= 1
                if not missing[user]:
                    ready[user] = max(end[need] for need in steps[user][0])
        return result, end


def kernel(
    img_in, txt_in, img_ids_in, txt_ids_in, scale_in, bias_in, img_out, txt_out,
    img_ref, txt_ref, img_ids_ref, txt_ids_ref, scale_ref, bias_ref, in_sems,
    imgs, txts, img_ids, txt_ids, img_col, txt_line, coef, img_part, txt_part,
    t1_send, t1_recv, t2_send, t2_recv, t3_send, t3_recv,
    core_send, core_recv, z_send, z_recv, send_sems, recv_sems,
):
    f32, bf16 = jnp.float32, jnp.bfloat16
    blk, grp = lax.axis_index("blk"), lax.axis_index("group")
    y, x_hi = lax.div(blk, 2), lax.rem(blk, 2)
    z, x_lo, core = lax.div(grp, 4), lax.rem(lax.div(grp, 2), 2), lax.rem(grp, 2)
    x = x_hi * 2 + x_lo

    def device(dx=0, dy=0, dz=0, dc=0):
        nx, ny, nz = lax.rem(x + dx + 4, 4), lax.rem(y + dy + 4, 4), lax.rem(z + dz + 8, 8)
        nc = lax.rem(core + dc, 2)
        return (ny * 2 + lax.div(nx, 2), (nz * 2 + lax.rem(nx, 2)) * 2 + nc)

    near = {
        "x+": device(dx=1), "x-": device(dx=-1), "y+": device(dy=1), "y-": device(dy=-1),
        "z+": device(dz=1), "z-": device(dz=-1), "core": device(dc=1),
        "x2": device(dx=2), "y2": device(dy=2), "z+2": device(dz=2), "z-2": device(dz=-2),
    }
    barrier = pltpu.get_barrier_semaphore()
    for there in near.values():
        pl.semaphore_signal(barrier, inc=1, device_id=there, device_id_type=MESH)

    loads = [
        pltpu.make_async_copy(src, dst, in_sems.at[number])
        for number, (src, dst) in enumerate([
            (img_in, img_ref), (txt_in, txt_ref), (img_ids_in, img_ids_ref), (txt_ids_in, txt_ids_ref),
            (scale_in, scale_ref), (bias_in, bias_ref),
        ])
    ]
    for load in loads:
        load.start()
    for load in loads:
        load.wait()
    own_img, own_txt = IMG_ROW[0, 0], {p: TXT_ROW[p, 0, 0] for p in "AB"}
    imgs[own_img:own_img + OWN, :] = unit_rows(img_ref[...])[0].astype(bf16)
    unit = unit_rows(txt_ref[...])[0].astype(bf16)
    txts[own_txt["A"]:own_txt["A"] + HALF, :] = unit[:HALF]
    txts[own_txt["B"]:own_txt["B"] + HALF, :] = unit[HALF:]
    line = img_ids_ref[...]
    img_ids[own_img // OWN] = jnp.concatenate([line] * 2, axis=1)
    line = txt_ids_ref[...]
    txt_ids[own_txt["A"] // HALF] = jnp.concatenate([line[:, :HALF]] * 4, axis=1)
    txt_ids[own_txt["B"] // HALF] = jnp.concatenate([line[:, HALF:]] * 4, axis=1)
    scale = jnp.exp(jnp.broadcast_to(scale_ref[...], (1, 256)))
    half_scale, half_bias = 0.5 * scale[:, 0:1], 0.5 * bias_ref[...]
    pl.semaphore_wait(barrier, len(near))

    plan = Plan()
    first_axis, second_axis = {"A": "x", "B": "y"}, {"A": "y", "B": "x"}
    halves = (0, 1)

    def move_text(p, src, dst, piece, to, needs):
        low = piece * QUART
        a, b = TXT_ROW[p, *src] + low, TXT_ROW[p, *dst] + low
        d, e = dst
        group = ("t", p, "far") if d == 2 else ("t", p, "rest") if (d == 1 and e > 1) or (d == 3 and e < 2) else None
        plan.copy(("t", p, *dst, piece), needs, QUART, txts.at[a:a + QUART, :], txts.at[b:b + QUART, :], to, group)

    def move_text_ids(p, src, dst, count, to, needs):
        a, b = TXT_ROW[p, *src] // HALF, TXT_ROW[p, *dst] // HALF
        group = {
            (0, 2): ("ti", p, 0), (0, 3): ("ti", p, 0), (2, 0): ("ti", p, 2), (2, 2): ("ti", p, 2),
            (1, 2): ("ti", p, "rest"), (3, 0): ("ti", p, "rest"),
        }.get(dst)
        plan.copy(("ti", p, *dst), needs, 1, txt_ids.at[a:a + count], txt_ids.at[b:b + count], to, group)

    def text_here(p, d, e, piece):
        return [] if (d, e) == (0, 0) else [("t", p, d, e, piece)]

    for p in "AB":
        one, two = first_axis[p], second_axis[p]
        for e, way, order in ((1, "+", (0, 1)), (3, "-", (1, 0))):
            for piece in order:
                move_text(p, (0, 0), (0, e), piece, one + way, [])
        for piece in halves:
            move_text(p, (0, 0), (0, 2), piece, one + "2", [])
        for e in range(4):
            for piece in halves:
                for d, way in ((1, "+"), (3, "-")):
                    move_text(p, (0, e), (d, e), piece, two + way, text_here(p, 0, e, piece))
                d, way = (1, "+") if e < 2 else (3, "-")
                move_text(p, (d, e), (2, e), piece, two + way, [("t", p, d, e, piece)])
        move_text_ids(p, (0, 0), (0, 1), 1, one + "+", [])
        move_text_ids(p, (0, 0), (0, 3), 1, one + "-", [])
        move_text_ids(p, (0, 0), (0, 2), 1, one + "2", [])
        for d, way in ((1, "+"), (3, "-")):
            move_text_ids(p, (0, 0), (d, 0), 2, two + way, [("ti", p, 0, 1)])
            move_text_ids(p, (0, 2), (d, 2), 2, two + way, [("ti", p, 0, 2), ("ti", p, 0, 3)])
        move_text_ids(p, (1, 0), (2, 0), 2, two + "+", [("ti", p, 1, 0)])
        move_text_ids(p, (3, 2), (2, 2), 2, two + "-", [("ti", p, 3, 2)])

    pieces = [(low, low + PIECE) for low in range(0, OWN, PIECE)]

    def move_image(src, dst, low, high, to, needs):
        a, b = IMG_ROW[src, 0], IMG_ROW[dst, 0]
        group = ("z", 4, "half", low // HALF) if dst == 4 else None
        plan.copy(
            ("z", dst, low), needs, high - low, imgs.at[a + low:a + high, :], imgs.at[b + low:b + high, :], to, group
        )

    for way, step in (("+", 1), ("-", -1)):
        for hops in range(1, 5):
            src, dst = (hops - 1 - hops // 4) * step % 8, hops * step % 8
            to = "z" + way + ("2" if hops == 4 else "")
            for low, high in pieces[::step]:
                if hops < 4 or (low < HALF) == (step > 0):
                    move_image(src, dst, low, high, to, [("z", src, low)] if src else [])
            if hops < 4 or step > 0:
                plan.copy(
                    ("zi", dst), [("zi", src)] if src else [], 1,
                    img_ids.at[IMG_ROW[src, 0] // OWN], img_ids.at[IMG_ROW[dst, 0] // OWN], to,
                )
    for dz in range(8):
        a, b = IMG_ROW[dz, 0], IMG_ROW[dz, 1]
        pair = min(dz, 8 - dz) or 1
        for half in halves:
            low, high = half * HALF, half * HALF + HALF
            plan.copy(
                ("c", dz, half), [("z", dz, at) for at, _ in pieces if low <= at < high and dz], HALF,
                imgs.at[a + low:a + high, :], imgs.at[b + low:b + high, :], "core", ("c", pair),
            )
        plan.copy(
            ("ci", dz), [("zi", dz)] if dz else [], 1, img_ids.at[a // OWN], img_ids.at[b // OWN], "core",
            ("ci", pair),
        )

    lane = lax.broadcasted_iota(jnp.int32, (1, 128), 1)

    def line_of_text(base):
        line = None
        for e in range(4):
            ids = txt_ids[base // HALF + e]
            line = ids if line is None else jnp.where(lane < HALF * e, line, ids)
        txt_line[:, base:base + 128] = line

    for base in range(0, ROWS, 128):
        ids = []
        for p, d, e in TXT_ORDER[base // HALF:base // HALF + 4]:
            if (d, e) != (0, 0):
                ids.append(("ti", p, d, e if d == 0 else e // 2 * 2))
        plan.work(("line", base), ids, 0.05, functools.partial(line_of_text, base))

    def column_of_images(row):
        place = row // OWN
        line = jnp.where(lane < OWN, img_ids[place], img_ids[place + 1])
        img_col[row:row + 128, :] = jnp.transpose(jnp.broadcast_to(line, (128, 128)))

    for row in range(0, ROWS, 128):
        ids = []
        for dz, cr in IMG_ORDER[row // OWN:row // OWN + 2]:
            ids += [("ci", dz)] if cr else [("zi", dz)] if dz else []
        plan.work(("column", row), ids, 0.1, functools.partial(column_of_images, row))

    def score_tile(r, high, t, right):
        scores = lax.dot_general(
            imgs[r:high, :], txts[t:right, :], (((1,), (1,)), ((), ())), preferred_element_type=f32
        )
        column = img_col[r:high, :]
        same = jnp.concatenate([column] * ((right - t) // 128), axis=1) == txt_line[:, t:right]
        value = 0.5 * jnp.tanh(half_scale * scores + half_bias) + jnp.where(same, -0.5, 0.5)
        coef[r:high, t:right] = value.astype(bf16)

    score_keys = []
    for r, high, t, right in SCORE_TILES:
        needs = [("column", row) for row in range(r, high, 128)] + [("line", base) for base in range(t, right, 128)]
        for dz, cr in IMG_ORDER[r // OWN:high // OWN]:
            needs += [("c", dz, half) for half in halves] if cr else [("z", dz, at) for at, _ in pieces if dz]
        for p, d, e in TXT_ORDER[t // HALF:right // HALF]:
            needs += [at for piece in halves for at in text_here(p, d, e, piece)]
        key = ("score", r, high, t, right)
        score_keys.append(key)
        cost = 0.12 + max(0.225, 0.00088 * (high - r)) * (right - t) / 256
        plan.work(key, needs, cost, functools.partial(score_tile, r, high, t, right))

    def img_terms(row):
        img_part[row:row + 128, :] = jnp.dot(coef[row:row + 128, :], txts[...], preferred_element_type=f32)

    def txt_terms(row):
        txt_part[row:row + 128, :] = lax.dot_general(
            coef[:, row:row + 128], imgs[...], (((0,), (0,)), ((), ())), preferred_element_type=f32
        )

    for row in range(0, ROWS, 128):
        needs = [key for key in score_keys if key[1] <= row < key[2]]
        plan.work(("img", row), needs, 0.37, functools.partial(img_terms, row))
        needs = [key for key in score_keys if key[3] <= row < key[4]]
        plan.work(("txt", row), needs, 0.38, functools.partial(txt_terms, row))

    def img_key(dz, cr):
        return ("img", IMG_ROW[dz, cr] // 128 * 128)

    def to_core(dz):
        row = IMG_ROW[dz, 1]
        core_send[OWN * dz:OWN * dz + OWN, :] = img_part[row:row + OWN, :].astype(bf16)

    def chip_sum(dz, low, high):
        row = IMG_ROW[dz, 0]
        return img_part[row + low:row + high, :] + core_recv[OWN * dz + low:OWN * dz + high, :].astype(f32)

    def z_out(dz, low, high, before):
        total = chip_sum(dz, low, high)
        for other in before:
            total = total + z_recv[OWN * other + low:OWN * other + high, :].astype(f32)
        z_send[OWN * dz + low:OWN * dz + high, :] = total.astype(bf16)

    for dz in range(8):
        rows = slice(OWN * dz, OWN * dz + OWN)
        plan.work(("to core", dz), [img_key(dz, 1)], 0.12, functools.partial(to_core, dz))
        plan.copy(("s", dz), [("to core", dz)], OWN, core_send.at[rows], core_recv.at[rows], "core", ("s", min(dz, 8 - dz)))
    for dz in (4, 3, 5, 2, 6, 1, 7):
        for low, high in pieces:
            way = "-" if dz < 4 or dz == 4 and low < HALF else "+"
            before = []
            if dz in (1, 2, 6, 7):
                before.append(dz + 1 if dz < 4 else dz - 1)
            if dz in (2, 6) and (low < HALF) == (dz == 2):
                before.append(4)
            needs = [img_key(dz, 0), ("s", dz)] + [("r", other, low) for other in before]
            plan.work(("z out", dz, low), needs, 0.08, functools.partial(z_out, dz, low, high, before))
            rows = slice(OWN * dz + low, OWN * dz + high)
            plan.copy(
                ("r", dz, low), [("z out", dz, low)], high - low, z_send.at[rows], z_recv.at[rows],
                "z" + way + ("2" if dz == 4 else ""),
                ("r", 1, "half", low // HALF) if dz in (1, 7) else None,
            )

    def t1_out(p, e, low, high):
        base, at = TXT_ROW[p, 2, e], 128 * "AB".index(p) + HALF * e
        t1_send[at + low:at + high, :] = txt_part[base + low:base + high, :].astype(bf16)

    def t2_out(p, d, e, low, high, added):
        base, at = TXT_ROW[p, d, e], 256 * "AB".index(p) + 128 * (d // 2) + HALF * e
        total = txt_part[base + low:base + high, :]
        if added:
            got = 128 * "AB".index(p) + HALF * e
            total = total + t1_recv[got + low:got + high, :].astype(f32)
        t2_send[at + low:at + high, :] = total.astype(bf16)

    def line_sum(p, e, low=0, high=HALF):
        base, at = TXT_ROW[p, 0, e], 256 * "AB".index(p) + HALF * e
        return (
            txt_part[base + low:base + high, :]
            + t2_recv[at + low:at + high, :].astype(f32)
            + t2_recv[at + 128 + low:at + 128 + high, :].astype(f32)
        )

    def t3_out(p, e, low, high):
        at = 96 * "AB".index(p) + HALF * (e - 1)
        t3_send[at + low:at + high, :] = line_sum(p, e, low, high).astype(bf16)

    def txt_key(p, d, e):
        return ("txt", TXT_ROW[p, d, e] // 128 * 128)

    def line_needs(p, e, low):
        return [txt_key(p, 0, e), ("t2", p, 1, e, low), ("t2", p, 3, e, low)]

    for p in "AB":
        one, two = first_axis[p], second_axis[p]
        for e in range(4):
            for low in (0, QUART):
                high = low + QUART
                at = 128 * "AB".index(p) + HALF * e
                rows = slice(at + low, at + high)
                plan.work(("t1 out", p, e, low), [txt_key(p, 2, e)], 0.06, functools.partial(t1_out, p, e, low, high))
                plan.copy(
                    ("t1", p, e, low), [("t1 out", p, e, low)], QUART, t1_send.at[rows], t1_recv.at[rows],
                    two + ("-" if e < 2 else "+"),
                )
                for d, way in ((1, "-"), (3, "+")):
                    added = (d == 1) == (e < 2)
                    at = 256 * "AB".index(p) + 128 * (d // 2) + HALF * e
                    rows = slice(at + low, at + high)
                    needs = [txt_key(p, d, e)] + ([("t1", p, e, low)] if added else [])
                    plan.work(
                        ("t2 out", p, d, e, low), needs, 0.07, functools.partial(t2_out, p, d, e, low, high, added)
                    )
                    plan.copy(
                        ("t2", p, d, e, low), [("t2 out", p, d, e, low)], QUART, t2_send.at[rows], t2_recv.at[rows],
                        two + way, ("t2", p, e, low),
                    )
                if e:
                    at = 96 * "AB".index(p) + HALF * (e - 1)
                    rows = slice(at + low, at + high)
                    plan.work(
                        ("t3 out", p, e, low), line_needs(p, e, low), 0.08, functools.partial(t3_out, p, e, low, high)
                    )
                    plan.copy(
                        ("t3", p, e, low), [("t3 out", p, e, low)], QUART, t3_send.at[rows], t3_recv.at[rows],
                        one + " -2+"[e], ("t3", p),
                    )

    def finish(embedding, total):
        unit, inverse = unit_rows(embedding)
        direction = scale[:, 0:1] * total
        return inverse * (direction - unit * jnp.sum(unit * direction, axis=1, keepdims=True))

    def finish_txt(p):
        low = HALF * "AB".index(p)
        total = line_sum(p, 0)
        for e in (1, 2, 3):
            at = 96 * "AB".index(p) + HALF * (e - 1)
            total = total + t3_recv[at:at + HALF, :].astype(f32)
        txt_out[low:low + HALF, :] = finish(txt_ref[low:low + HALF, :], total)

    def finish_img(low, high):
        total = chip_sum(0, low, high)
        for dz in (1, 7):
            total = total + z_recv[OWN * dz + low:OWN * dz + high, :].astype(f32)
        img_out[low:high, :] = finish(img_ref[low:high, :], total)

    for p in "AB":
        needs = [need for low in (0, QUART) for need in line_needs(p, 0, low) + [("t3", p, e, low) for e in (1, 2, 3)]]
        plan.work(("end", p), needs, 0.2, functools.partial(finish_txt, p))
    for low in (HALF, 0):
        needs = [img_key(0, 0), ("s", 0), ("r", 1, low)]
        plan.work(("end", low), needs, 0.15, functools.partial(finish_img, low, low + HALF))

    arrives = {group: recv_sems.at[number] for number, group in enumerate(plan.groups)}
    sent = []

    def whole(rows, ids):
        return txt_ids.at[0:rows] if ids else imgs.at[0:rows, :]

    def await_copy(ref, sem):
        pltpu.make_async_copy(ref, ref, sem).wait()

    here = set()
    for key in plan.order()[0]:
        needs, _, run, links, _ = plan.steps[key]
        for need in needs:
            group = plan.group_of.get(need)
            if group is None or group in here:
                continue
            here.add(group)
            landed = [plan.steps[member][2][1] for member in plan.groups[group]]
            ids = landed[0].dtype != bf16
            await_copy(whole(sum(1 if ref.ndim == 2 and ids else ref.shape[0] for ref in landed), ids), arrives[group])
        if links is None:
            run()
            continue
        src, dst, to = run
        ids = src.dtype != bf16
        rows = 1 if src.ndim == 2 and ids else src.shape[0]
        open_sems = [entry for entry in sent if entry[0] == ids and entry[1] + rows <= (32 if ids else ROWS)]
        if not open_sems:
            open_sems = [[ids, 0, send_sems.at[len(sent)]]]
            sent.append(open_sems[0])
        open_sems[0][1] += rows
        pltpu.make_async_remote_copy(
            src_ref=src, dst_ref=dst, send_sem=open_sems[0][2], recv_sem=arrives[plan.group_of[key]],
            device_id=near[to], device_id_type=MESH,
        ).start()
    for ids, rows, sem in sent:
        await_copy(whole(rows, ids), sem)


def write_out(img_grad, txt_grad, img_out, txt_out, sems):
    copies = [
        pltpu.make_async_copy(src, dst, sems.at[number])
        for number, (src, dst) in enumerate([(img_grad, img_out), (txt_grad, txt_out)])
    ]
    for copy in copies:
        copy.start()
    for copy in copies:
        copy.wait()


def body(img_emb, txt_emb, img_ids, txt_ids, scale_logarithm, bias):
    f32, bf16, i32 = jnp.float32, jnp.bfloat16, jnp.int32
    anywhere = pl.BlockSpec(memory_space=pl.ANY)
    in_vmem = pl.BlockSpec(memory_space=pltpu.VMEM)
    grads = pl.pallas_call(
        kernel,
        out_shape=(pltpu.VMEM((OWN, D), f32), pltpu.VMEM((OWN, D), f32)),
        in_specs=[anywhere] * 6,
        out_specs=(in_vmem, in_vmem),
        scratch_shapes=[
            pltpu.VMEM((OWN, D), bf16),
            pltpu.VMEM((OWN, D), bf16),
            pltpu.VMEM((1, OWN), i32),
            pltpu.VMEM((1, OWN), i32),
            pltpu.VMEM((1, 1), f32),
            pltpu.VMEM((1, 1), f32),
            pltpu.SemaphoreType.DMA((6,)),
            pltpu.VMEM((ROWS, D), bf16),
            pltpu.VMEM((ROWS, D), bf16),
            pltpu.VMEM((16, 1, 128), i32),
            pltpu.VMEM((32, 1, 128), i32),
            pltpu.VMEM((ROWS, 128), i32),
            pltpu.VMEM((1, ROWS), i32),
            pltpu.VMEM((ROWS, ROWS), bf16),
            pltpu.VMEM((ROWS, D), f32),
            pltpu.VMEM((ROWS, D), f32),
            pltpu.VMEM((256, D), bf16),
            pltpu.VMEM((256, D), bf16),
            pltpu.VMEM((512, D), bf16),
            pltpu.VMEM((512, D), bf16),
            pltpu.VMEM((192, D), bf16),
            pltpu.VMEM((192, D), bf16),
            pltpu.VMEM((512, D), bf16),
            pltpu.VMEM((512, D), bf16),
            pltpu.VMEM((512, D), bf16),
            pltpu.VMEM((512, D), bf16),
            pltpu.SemaphoreType.DMA((N_SENT,)),
            pltpu.SemaphoreType.DMA((N_ARRIVALS,)),
        ],
        compiler_params=pltpu.CompilerParams(
            collective_id=0, has_side_effects=True, vmem_limit_bytes=56 * 1024 * 1024
        ),
        cost_estimate=pl.CostEstimate(flops=7247757312, bytes_accessed=900000, transcendentals=1048576),
    )(img_emb, txt_emb, img_ids.reshape(1, OWN), txt_ids.reshape(1, OWN),
      scale_logarithm.reshape(1, 1), bias.reshape(1, 1))
    return pl.pallas_call(
        write_out,
        out_shape=(jax.ShapeDtypeStruct((OWN, D), f32), jax.ShapeDtypeStruct((OWN, D), f32)),
        in_specs=[in_vmem, in_vmem],
        out_specs=(anywhere, anywhere),
        scratch_shapes=[pltpu.SemaphoreType.DMA((2,))],
    )(*[pltpu.with_memory_space_constraint(grad, pltpu.VMEM) for grad in grads])


def solution(mesh):
    split = P(("blk", "group"), None)
    ids = P(("blk", "group"))
    return jax.shard_map(
        body,
        mesh=mesh,
        in_specs=(split, split, ids, ids, P(), P()),
        out_specs=(split, split),
        check_vma=False,
    )
```

```python
import functools

import jax
import jax.numpy as jnp
from jax import lax
from jax.experimental import pallas as pl
from jax.experimental.pallas import tpu as pltpu
from jax.sharding import PartitionSpec as P

MESH = pl.DeviceIdType.MESH
D = 1152
OWN = 64
HALF = 32
QUART = 16
ROWS = 1024
PIECE = 16
N_ARRIVALS = 146
N_SENT = 6

LINK_ROW, CORE_ROW, LINK_WAIT, CORE_WAIT, ISSUE, QUEUE = 0.0493, 0.0035, 2.4, 2.4, 0.02, 1.6
ROUTE = {
    **{way: ((way,), 1, 0.0) for way in ("x+", "x-", "y+", "y-", "z+", "z-", "core")},
    "x2": (("x+", "x-"), 1, 0.6), "y2": (("y+", "y-"), 1, 0.6), "z+2": (("z+",), 2, 0.6), "z-2": (("z-",), 2, 0.6),
}

IMG_ORDER = [
    (4, 1), (4, 0),
    (3, 1), (5, 1), (3, 0), (5, 0),
    (2, 1), (6, 1), (2, 0), (6, 0),
    (1, 1), (7, 1), (0, 1), (1, 0), (7, 0), (0, 0),
]
IMG_ROW = {key: OWN * place for place, key in enumerate(IMG_ORDER)}

TXT_ORDER = (
    [(p, 2, e) for p in "AB" for e in range(4)]
    + [(p, d, e) for p in "AB" for d, e in ((1, 2), (1, 3), (3, 0), (3, 1))]
    + [(p, d, e) for p in "AB" for d, e in ((1, 0), (1, 1), (3, 2), (3, 3))]
    + [(p, 0, e) for p in "AB" for e in range(4)]
)
TXT_ROW = {key: HALF * place for place, key in enumerate(TXT_ORDER)}


SCORE_TILES = [
    (640, 1024, 768, 1024), (384, 640, 768, 1024), (128, 384, 768, 1024),
    (384, 1024, 512, 768), (128, 384, 512, 768),
    (384, 1024, 256, 512), (128, 384, 256, 512),
    (128, 1024, 0, 256),
    (0, 128, 0, 1024),
]


def unit_rows(embedding):
    widened = embedding.astype(jnp.float32)
    inverse = lax.rsqrt(jnp.sum(widened * widened, axis=1, keepdims=True) + 1e-06)
    return widened * inverse, inverse


class Plan:
    def __init__(self):
        self.steps, self.group_of, self.groups = {}, {}, {}

    def work(self, key, needs, cost, run):
        self.steps[key] = (tuple(needs), cost, run, None, 0.0)

    def copy(self, key, needs, rows, src, dst, to, group=None):
        links, times, more = ROUTE[to]
        length = rows * times * (CORE_ROW if to == "core" else LINK_ROW)
        wait = CORE_WAIT if to == "core" else LINK_WAIT + more
        self.steps[key] = (tuple(needs), length, (src, dst, to), links, wait)
        self.group_of[key] = group or key
        self.groups.setdefault(group or key, []).append(key)

    def all_needs(self, key):
        result = []
        for need in self.steps[key][0]:
            result += self.groups[self.group_of[need]] if need in self.group_of else [need]
        return tuple(dict.fromkeys(result))

    def order(self):
        steps = {key: (self.all_needs(key), *step[1:]) for key, step in self.steps.items()}
        users = {key: [] for key in steps}
        for key, step in steps.items():
            for need in step[0]:
                users[need].append(key)
        left = {}

        def to_end(key):
            if key not in left:
                left[key] = steps[key][1] + steps[key][4] + max([to_end(user) for user in users[key]], default=0.0)
            return left[key]

        rank = {key: (-to_end(key), number) for number, key in enumerate(steps)}
        now, ready, free, end, result = 0.0, {}, {}, {}, []
        missing = {key: len(step[0]) for key, step in steps.items()}
        for key in steps:
            if not missing[key]:
                ready[key] = 0.0
        while ready:
            def opens(key):
                links = steps[key][3] or ()
                return max([ready[key]] + [free.get(link, 0.0) - QUEUE for link in links])

            now = max(now, min(opens(key) for key in ready))
            able = [key for key in ready if opens(key) <= now]
            key = min(able, key=lambda key: (steps[key][3] is None, rank[key]))
            del ready[key]
            needs, length, run, links, wait = steps[key]
            if links is None:
                now += length
                end[key] = now
            else:
                now += ISSUE
                for link in links:
                    free[link] = max(now, free.get(link, 0.0)) + length
                end[key] = max(free[link] for link in links) + wait
            result.append(key)
            for user in users[key]:
                missing[user] -= 1
                if not missing[user]:
                    ready[user] = max(end[need] for need in steps[user][0])
        return result, end


def kernel(
    img_in, txt_in, img_ids_in, txt_ids_in, scale_in, bias_in, img_out, txt_out,
    img_ref, txt_ref, img_ids_ref, txt_ids_ref, scale_ref, bias_ref, in_sems,
    imgs, txts, img_ids, txt_ids, img_col, txt_line, coef, img_part, txt_part,
    t1_send, t1_recv, t2_send, t2_recv, t3_send, t3_recv,
    core_send, core_recv, z_send, z_recv, send_sems, recv_sems,
):
    f32, bf16 = jnp.float32, jnp.bfloat16
    blk, grp = lax.axis_index("blk"), lax.axis_index("group")
    y, x_hi = lax.div(blk, 2), lax.rem(blk, 2)
    z, x_lo, core = lax.div(grp, 4), lax.rem(lax.div(grp, 2), 2), lax.rem(grp, 2)
    x = x_hi * 2 + x_lo

    def device(dx=0, dy=0, dz=0, dc=0):
        nx, ny, nz = lax.rem(x + dx + 4, 4), lax.rem(y + dy + 4, 4), lax.rem(z + dz + 8, 8)
        nc = lax.rem(core + dc, 2)
        return (ny * 2 + lax.div(nx, 2), (nz * 2 + lax.rem(nx, 2)) * 2 + nc)

    near = {
        "x+": device(dx=1), "x-": device(dx=-1), "y+": device(dy=1), "y-": device(dy=-1),
        "z+": device(dz=1), "z-": device(dz=-1), "core": device(dc=1),
        "x2": device(dx=2), "y2": device(dy=2), "z+2": device(dz=2), "z-2": device(dz=-2),
    }
    barrier = pltpu.get_barrier_semaphore()
    for there in near.values():
        pl.semaphore_signal(barrier, inc=1, device_id=there, device_id_type=MESH)

    loads = [
        pltpu.make_async_copy(src, dst, in_sems.at[number])
        for number, (src, dst) in enumerate([
            (img_in, img_ref), (txt_in, txt_ref), (img_ids_in, img_ids_ref), (txt_ids_in, txt_ids_ref),
            (scale_in, scale_ref), (bias_in, bias_ref),
        ])
    ]
    for load in loads:
        load.start()
    for load in loads:
        load.wait()
    own_img, own_txt = IMG_ROW[0, 0], {p: TXT_ROW[p, 0, 0] for p in "AB"}
    imgs[own_img:own_img + OWN, :] = unit_rows(img_ref[...])[0].astype(bf16)
    unit = unit_rows(txt_ref[...])[0].astype(bf16)
    txts[own_txt["A"]:own_txt["A"] + HALF, :] = unit[:HALF]
    txts[own_txt["B"]:own_txt["B"] + HALF, :] = unit[HALF:]
    line = img_ids_ref[...]
    img_ids[own_img // OWN] = jnp.concatenate([line] * 2, axis=1)
    line = txt_ids_ref[...]
    txt_ids[own_txt["A"] // HALF] = jnp.concatenate([line[:, :HALF]] * 4, axis=1)
    txt_ids[own_txt["B"] // HALF] = jnp.concatenate([line[:, HALF:]] * 4, axis=1)
    scale = jnp.exp(jnp.broadcast_to(scale_ref[...], (1, 256)))
    half_scale, half_bias = 0.5 * scale[:, 0:1], 0.5 * bias_ref[...]
    pl.semaphore_wait(barrier, len(near))

    plan = Plan()
    first_axis, second_axis = {"A": "x", "B": "y"}, {"A": "y", "B": "x"}
    halves = (0, 1)

    def move_text(p, src, dst, piece, to, needs):
        low = piece * QUART
        a, b = TXT_ROW[p, *src] + low, TXT_ROW[p, *dst] + low
        d, e = dst
        group = ("t", p, "far") if d == 2 else ("t", p, "rest") if (d == 1 and e > 1) or (d == 3 and e < 2) else None
        plan.copy(("t", p, *dst, piece), needs, QUART, txts.at[a:a + QUART, :], txts.at[b:b + QUART, :], to, group)

    def move_text_ids(p, src, dst, count, to, needs):
        a, b = TXT_ROW[p, *src] // HALF, TXT_ROW[p, *dst] // HALF
        group = {
            (0, 2): ("ti", p, 0), (0, 3): ("ti", p, 0), (2, 0): ("ti", p, 2), (2, 2): ("ti", p, 2),
            (1, 2): ("ti", p, "rest"), (3, 0): ("ti", p, "rest"),
        }.get(dst)
        plan.copy(("ti", p, *dst), needs, 1, txt_ids.at[a:a + count], txt_ids.at[b:b + count], to, group)

    def text_here(p, d, e, piece):
        return [] if (d, e) == (0, 0) else [("t", p, d, e, piece)]

    for p in "AB":
        one, two = first_axis[p], second_axis[p]
        for e, way, order in ((1, "+", (0, 1)), (3, "-", (1, 0))):
            for piece in order:
                move_text(p, (0, 0), (0, e), piece, one + way, [])
        for piece in halves:
            move_text(p, (0, 0), (0, 2), piece, one + "2", [])
        for e in range(4):
            for piece in halves:
                for d, way in ((1, "+"), (3, "-")):
                    move_text(p, (0, e), (d, e), piece, two + way, text_here(p, 0, e, piece))
                d, way = (1, "+") if e < 2 else (3, "-")
                move_text(p, (d, e), (2, e), piece, two + way, [("t", p, d, e, piece)])
        move_text_ids(p, (0, 0), (0, 1), 1, one + "+", [])
        move_text_ids(p, (0, 0), (0, 3), 1, one + "-", [])
        move_text_ids(p, (0, 0), (0, 2), 1, one + "2", [])
        for d, way in ((1, "+"), (3, "-")):
            move_text_ids(p, (0, 0), (d, 0), 2, two + way, [("ti", p, 0, 1)])
            move_text_ids(p, (0, 2), (d, 2), 2, two + way, [("ti", p, 0, 2), ("ti", p, 0, 3)])
        move_text_ids(p, (1, 0), (2, 0), 2, two + "+", [("ti", p, 1, 0)])
        move_text_ids(p, (3, 2), (2, 2), 2, two + "-", [("ti", p, 3, 2)])

    pieces = [(low, low + PIECE) for low in range(0, OWN, PIECE)]

    def move_image(src, dst, low, high, to, needs):
        a, b = IMG_ROW[src, 0], IMG_ROW[dst, 0]
        group = ("z", 4, "half", low // HALF) if dst == 4 else None
        plan.copy(
            ("z", dst, low), needs, high - low, imgs.at[a + low:a + high, :], imgs.at[b + low:b + high, :], to, group
        )

    for way, step in (("+", 1), ("-", -1)):
        for hops in range(1, 5):
            src, dst = (hops - 1 - hops // 4) * step % 8, hops * step % 8
            to = "z" + way + ("2" if hops == 4 else "")
            for low, high in pieces[::step]:
                if hops < 4 or (low < HALF) == (step > 0):
                    move_image(src, dst, low, high, to, [("z", src, low)] if src else [])
            if hops < 4 or step > 0:
                plan.copy(
                    ("zi", dst), [("zi", src)] if src else [], 1,
                    img_ids.at[IMG_ROW[src, 0] // OWN], img_ids.at[IMG_ROW[dst, 0] // OWN], to,
                )
    for dz in range(8):
        a, b = IMG_ROW[dz, 0], IMG_ROW[dz, 1]
        pair = min(dz, 8 - dz) or 1
        for half in halves:
            low, high = half * HALF, half * HALF + HALF
            plan.copy(
                ("c", dz, half), [("z", dz, at) for at, _ in pieces if low <= at < high and dz], HALF,
                imgs.at[a + low:a + high, :], imgs.at[b + low:b + high, :], "core", ("c", pair),
            )
        plan.copy(
            ("ci", dz), [("zi", dz)] if dz else [], 1, img_ids.at[a // OWN], img_ids.at[b // OWN], "core",
            ("ci", pair),
        )

    lane = lax.broadcasted_iota(jnp.int32, (1, 128), 1)

    def line_of_text(base):
        line = None
        for e in range(4):
            ids = txt_ids[base // HALF + e]
            line = ids if line is None else jnp.where(lane < HALF * e, line, ids)
        txt_line[:, base:base + 128] = line

    for base in range(0, ROWS, 128):
        ids = []
        for p, d, e in TXT_ORDER[base // HALF:base // HALF + 4]:
            if (d, e) != (0, 0):
                ids.append(("ti", p, d, e if d == 0 else e // 2 * 2))
        plan.work(("line", base), ids, 0.05, functools.partial(line_of_text, base))

    def column_of_images(row):
        place = row // OWN
        line = jnp.where(lane < OWN, img_ids[place], img_ids[place + 1])
        img_col[row:row + 128, :] = jnp.transpose(jnp.broadcast_to(line, (128, 128)))

    for row in range(0, ROWS, 128):
        ids = []
        for dz, cr in IMG_ORDER[row // OWN:row // OWN + 2]:
            ids += [("ci", dz)] if cr else [("zi", dz)] if dz else []
        plan.work(("column", row), ids, 0.1, functools.partial(column_of_images, row))

    def score_tile(r, high, t, right):
        scores = lax.dot_general(
            imgs[r:high, :], txts[t:right, :], (((1,), (1,)), ((), ())), preferred_element_type=f32
        )
        column = img_col[r:high, :]
        same = jnp.concatenate([column] * ((right - t) // 128), axis=1) == txt_line[:, t:right]
        value = 0.5 * jnp.tanh(half_scale * scores + half_bias) + jnp.where(same, -0.5, 0.5)
        coef[r:high, t:right] = value.astype(bf16)

    score_keys = []
    for r, high, t, right in SCORE_TILES:
        needs = [("column", row) for row in range(r, high, 128)] + [("line", base) for base in range(t, right, 128)]
        for dz, cr in IMG_ORDER[r // OWN:high // OWN]:
            needs += [("c", dz, half) for half in halves] if cr else [("z", dz, at) for at, _ in pieces if dz]
        for p, d, e in TXT_ORDER[t // HALF:right // HALF]:
            needs += [at for piece in halves for at in text_here(p, d, e, piece)]
        key = ("score", r, high, t, right)
        score_keys.append(key)
        cost = 0.08 + max(0.15, 0.0006 * (high - r)) * (right - t) / 256
        plan.work(key, needs, cost, functools.partial(score_tile, r, high, t, right))

    def img_terms(row):
        img_part[row:row + 128, :] = jnp.dot(coef[row:row + 128, :], txts[...], preferred_element_type=f32)

    def txt_terms(row):
        txt_part[row:row + 128, :] = lax.dot_general(
            coef[:, row:row + 128], imgs[...], (((0,), (0,)), ((), ())), preferred_element_type=f32
        )

    for row in range(0, ROWS, 128):
        needs = [key for key in score_keys if key[1] <= row < key[2]]
        plan.work(("img", row), needs, 0.41, functools.partial(img_terms, row))
        needs = [key for key in score_keys if key[3] <= row < key[4]]
        plan.work(("txt", row), needs, 0.42, functools.partial(txt_terms, row))

    def img_key(dz, cr):
        return ("img", IMG_ROW[dz, cr] // 128 * 128)

    def to_core(dz):
        row = IMG_ROW[dz, 1]
        core_send[OWN * dz:OWN * dz + OWN, :] = img_part[row:row + OWN, :].astype(bf16)

    def chip_sum(dz, low, high):
        row = IMG_ROW[dz, 0]
        return img_part[row + low:row + high, :] + core_recv[OWN * dz + low:OWN * dz + high, :].astype(f32)

    def z_out(dz, low, high, before):
        total = chip_sum(dz, low, high)
        for other in before:
            total = total + z_recv[OWN * other + low:OWN * other + high, :].astype(f32)
        z_send[OWN * dz + low:OWN * dz + high, :] = total.astype(bf16)

    for dz in range(8):
        rows = slice(OWN * dz, OWN * dz + OWN)
        plan.work(("to core", dz), [img_key(dz, 1)], 0.04, functools.partial(to_core, dz))
        plan.copy(("s", dz), [("to core", dz)], OWN, core_send.at[rows], core_recv.at[rows], "core", ("s", min(dz, 8 - dz)))
    for dz in (4, 3, 5, 2, 6, 1, 7):
        for low, high in pieces:
            way = "-" if dz < 4 or dz == 4 and low < HALF else "+"
            before = []
            if dz in (1, 2, 6, 7):
                before.append(dz + 1 if dz < 4 else dz - 1)
            if dz in (2, 6) and (low < HALF) == (dz == 2):
                before.append(4)
            needs = [img_key(dz, 0), ("s", dz)] + [("r", other, low) for other in before]
            plan.work(("z out", dz, low), needs, 0.03, functools.partial(z_out, dz, low, high, before))
            rows = slice(OWN * dz + low, OWN * dz + high)
            plan.copy(
                ("r", dz, low), [("z out", dz, low)], high - low, z_send.at[rows], z_recv.at[rows],
                "z" + way + ("2" if dz == 4 else ""),
                ("r", 1, "half", low // HALF) if dz in (1, 7) else None,
            )

    def t1_out(p, e, low, high):
        base, at = TXT_ROW[p, 2, e], 128 * "AB".index(p) + HALF * e
        t1_send[at + low:at + high, :] = txt_part[base + low:base + high, :].astype(bf16)

    def t2_out(p, d, e, low, high, added):
        base, at = TXT_ROW[p, d, e], 256 * "AB".index(p) + 128 * (d // 2) + HALF * e
        total = txt_part[base + low:base + high, :]
        if added:
            got = 128 * "AB".index(p) + HALF * e
            total = total + t1_recv[got + low:got + high, :].astype(f32)
        t2_send[at + low:at + high, :] = total.astype(bf16)

    def line_sum(p, e, low=0, high=HALF):
        base, at = TXT_ROW[p, 0, e], 256 * "AB".index(p) + HALF * e
        return (
            txt_part[base + low:base + high, :]
            + t2_recv[at + low:at + high, :].astype(f32)
            + t2_recv[at + 128 + low:at + 128 + high, :].astype(f32)
        )

    def t3_out(p, e, low, high):
        at = 96 * "AB".index(p) + HALF * (e - 1)
        t3_send[at + low:at + high, :] = line_sum(p, e, low, high).astype(bf16)

    def txt_key(p, d, e):
        return ("txt", TXT_ROW[p, d, e] // 128 * 128)

    def line_needs(p, e, low):
        return [txt_key(p, 0, e), ("t2", p, 1, e, low), ("t2", p, 3, e, low)]

    for p in "AB":
        one, two = first_axis[p], second_axis[p]
        for e in range(4):
            for low in (0, QUART):
                high = low + QUART
                at = 128 * "AB".index(p) + HALF * e
                rows = slice(at + low, at + high)
                plan.work(("t1 out", p, e, low), [txt_key(p, 2, e)], 0.02, functools.partial(t1_out, p, e, low, high))
                plan.copy(
                    ("t1", p, e, low), [("t1 out", p, e, low)], QUART, t1_send.at[rows], t1_recv.at[rows],
                    two + ("-" if e < 2 else "+"),
                )
                for d, way in ((1, "-"), (3, "+")):
                    added = (d == 1) == (e < 2)
                    at = 256 * "AB".index(p) + 128 * (d // 2) + HALF * e
                    rows = slice(at + low, at + high)
                    needs = [txt_key(p, d, e)] + ([("t1", p, e, low)] if added else [])
                    plan.work(
                        ("t2 out", p, d, e, low), needs, 0.03, functools.partial(t2_out, p, d, e, low, high, added)
                    )
                    plan.copy(
                        ("t2", p, d, e, low), [("t2 out", p, d, e, low)], QUART, t2_send.at[rows], t2_recv.at[rows],
                        two + way, ("t2", p, e, low),
                    )
                if e:
                    at = 96 * "AB".index(p) + HALF * (e - 1)
                    rows = slice(at + low, at + high)
                    plan.work(
                        ("t3 out", p, e, low), line_needs(p, e, low), 0.03, functools.partial(t3_out, p, e, low, high)
                    )
                    plan.copy(
                        ("t3", p, e, low), [("t3 out", p, e, low)], QUART, t3_send.at[rows], t3_recv.at[rows],
                        one + " -2+"[e], ("t3", p),
                    )

    def finish(embedding, total):
        unit, inverse = unit_rows(embedding)
        direction = scale[:, 0:1] * total
        return inverse * (direction - unit * jnp.sum(unit * direction, axis=1, keepdims=True))

    def finish_txt(p):
        low = HALF * "AB".index(p)
        total = line_sum(p, 0)
        for e in (1, 2, 3):
            at = 96 * "AB".index(p) + HALF * (e - 1)
            total = total + t3_recv[at:at + HALF, :].astype(f32)
        txt_out[low:low + HALF, :] = finish(txt_ref[low:low + HALF, :], total)

    def finish_img(low, high):
        total = chip_sum(0, low, high)
        for dz in (1, 7):
            total = total + z_recv[OWN * dz + low:OWN * dz + high, :].astype(f32)
        img_out[low:high, :] = finish(img_ref[low:high, :], total)

    for p in "AB":
        needs = [need for low in (0, QUART) for need in line_needs(p, 0, low) + [("t3", p, e, low) for e in (1, 2, 3)]]
        plan.work(("end", p), needs, 0.2, functools.partial(finish_txt, p))
    for low in (HALF, 0):
        needs = [img_key(0, 0), ("s", 0), ("r", 1, low)]
        plan.work(("end", low), needs, 0.15, functools.partial(finish_img, low, low + HALF))

    arrives = {group: recv_sems.at[number] for number, group in enumerate(plan.groups)}
    sent = []

    def whole(rows, ids):
        return txt_ids.at[0:rows] if ids else imgs.at[0:rows, :]

    def await_copy(ref, sem):
        pltpu.make_async_copy(ref, ref, sem).wait()

    here = set()
    for key in plan.order()[0]:
        needs, _, run, links, _ = plan.steps[key]
        for need in needs:
            group = plan.group_of.get(need)
            if group is None or group in here:
                continue
            here.add(group)
            landed = [plan.steps[member][2][1] for member in plan.groups[group]]
            ids = landed[0].dtype != bf16
            await_copy(whole(sum(1 if ref.ndim == 2 and ids else ref.shape[0] for ref in landed), ids), arrives[group])
        if links is None:
            run()
            continue
        src, dst, to = run
        ids = src.dtype != bf16
        rows = 1 if src.ndim == 2 and ids else src.shape[0]
        open_sems = [entry for entry in sent if entry[0] == ids and entry[1] + rows <= (32 if ids else ROWS)]
        if not open_sems:
            open_sems = [[ids, 0, send_sems.at[len(sent)]]]
            sent.append(open_sems[0])
        open_sems[0][1] += rows
        pltpu.make_async_remote_copy(
            src_ref=src, dst_ref=dst, send_sem=open_sems[0][2], recv_sem=arrives[plan.group_of[key]],
            device_id=near[to], device_id_type=MESH,
        ).start()
    for ids, rows, sem in sent:
        await_copy(whole(rows, ids), sem)


def write_out(img_grad, txt_grad, img_out, txt_out, sems):
    copies = [
        pltpu.make_async_copy(src, dst, sems.at[number])
        for number, (src, dst) in enumerate([(img_grad, img_out), (txt_grad, txt_out)])
    ]
    for copy in copies:
        copy.start()
    for copy in copies:
        copy.wait()


def body(img_emb, txt_emb, img_ids, txt_ids, scale_logarithm, bias):
    f32, bf16, i32 = jnp.float32, jnp.bfloat16, jnp.int32
    anywhere = pl.BlockSpec(memory_space=pl.ANY)
    in_vmem = pl.BlockSpec(memory_space=pltpu.VMEM)
    grads = pl.pallas_call(
        kernel,
        out_shape=(pltpu.VMEM((OWN, D), f32), pltpu.VMEM((OWN, D), f32)),
        in_specs=[anywhere] * 6,
        out_specs=(in_vmem, in_vmem),
        scratch_shapes=[
            pltpu.VMEM((OWN, D), bf16),
            pltpu.VMEM((OWN, D), bf16),
            pltpu.VMEM((1, OWN), i32),
            pltpu.VMEM((1, OWN), i32),
            pltpu.VMEM((1, 1), f32),
            pltpu.VMEM((1, 1), f32),
            pltpu.SemaphoreType.DMA((6,)),
            pltpu.VMEM((ROWS, D), bf16),
            pltpu.VMEM((ROWS, D), bf16),
            pltpu.VMEM((16, 1, 128), i32),
            pltpu.VMEM((32, 1, 128), i32),
            pltpu.VMEM((ROWS, 128), i32),
            pltpu.VMEM((1, ROWS), i32),
            pltpu.VMEM((ROWS, ROWS), bf16),
            pltpu.VMEM((ROWS, D), f32),
            pltpu.VMEM((ROWS, D), f32),
            pltpu.VMEM((256, D), bf16),
            pltpu.VMEM((256, D), bf16),
            pltpu.VMEM((512, D), bf16),
            pltpu.VMEM((512, D), bf16),
            pltpu.VMEM((192, D), bf16),
            pltpu.VMEM((192, D), bf16),
            pltpu.VMEM((512, D), bf16),
            pltpu.VMEM((512, D), bf16),
            pltpu.VMEM((512, D), bf16),
            pltpu.VMEM((512, D), bf16),
            pltpu.SemaphoreType.DMA((N_SENT,)),
            pltpu.SemaphoreType.DMA((N_ARRIVALS,)),
        ],
        compiler_params=pltpu.CompilerParams(
            collective_id=0, has_side_effects=True, vmem_limit_bytes=56 * 1024 * 1024
        ),
        cost_estimate=pl.CostEstimate(flops=7247757312, bytes_accessed=900000, transcendentals=1048576),
    )(img_emb, txt_emb, img_ids.reshape(1, OWN), txt_ids.reshape(1, OWN),
      scale_logarithm.reshape(1, 1), bias.reshape(1, 1))
    return pl.pallas_call(
        write_out,
        out_shape=(jax.ShapeDtypeStruct((OWN, D), f32), jax.ShapeDtypeStruct((OWN, D), f32)),
        in_specs=[in_vmem, in_vmem],
        out_specs=(anywhere, anywhere),
        scratch_shapes=[pltpu.SemaphoreType.DMA((2,))],
    )(*[pltpu.with_memory_space_constraint(grad, pltpu.VMEM) for grad in grads])


def solution(mesh):
    split = P(("blk", "group"), None)
    ids = P(("blk", "group"))
    return jax.shard_map(
        body,
        mesh=mesh,
        in_specs=(split, split, ids, ids, P(), P()),
        out_specs=(split, split),
        check_vma=False,
    )
```

```python
import functools

import jax
import jax.numpy as jnp
from jax import lax
from jax.experimental import pallas as pl
from jax.experimental.pallas import tpu as pltpu
from jax.sharding import PartitionSpec as P

MESH = pl.DeviceIdType.MESH
D = 1152
OWN = 64
HALF = 32
QUART = 16
ROWS = 1024
PIECE = 16
N_ARRIVALS = 146
N_SENT = 6

LINK_ROW, CORE_ROW, LINK_WAIT, CORE_WAIT, ISSUE, QUEUE = 0.0493, 0.0035, 2.4, 2.4, 0.02, 1.6
ROUTE = {
    **{way: ((way,), 1, 0.0) for way in ("x+", "x-", "y+", "y-", "z+", "z-", "core")},
    "x2": (("x+", "x-"), 1, 0.6), "y2": (("y+", "y-"), 1, 0.6), "z+2": (("z+",), 2, 0.6), "z-2": (("z-",), 2, 0.6),
}

IMG_ORDER = [
    (4, 1), (4, 0),
    (3, 1), (5, 1), (3, 0), (5, 0),
    (2, 1), (6, 1), (2, 0), (6, 0),
    (1, 1), (7, 1), (0, 1), (1, 0), (7, 0), (0, 0),
]
IMG_ROW = {key: OWN * place for place, key in enumerate(IMG_ORDER)}

TXT_ORDER = (
    [(p, 2, e) for p in "AB" for e in range(4)]
    + [(p, d, e) for p in "AB" for d, e in ((1, 2), (1, 3), (3, 0), (3, 1))]
    + [(p, d, e) for p in "AB" for d, e in ((1, 0), (1, 1), (3, 2), (3, 3))]
    + [(p, 0, e) for p in "AB" for e in range(4)]
)
TXT_ROW = {key: HALF * place for place, key in enumerate(TXT_ORDER)}


SCORE_TILES = [
    (640, 1024, 768, 1024), (384, 640, 768, 1024), (128, 384, 768, 1024),
    (384, 1024, 512, 768), (128, 384, 512, 768),
    (384, 1024, 256, 512), (128, 384, 256, 512),
    (128, 1024, 0, 256),
    (0, 128, 0, 1024),
]


def unit_rows(embedding):
    widened = embedding.astype(jnp.float32)
    inverse = lax.rsqrt(jnp.sum(widened * widened, axis=1, keepdims=True) + 1e-06)
    return widened * inverse, inverse


class Plan:
    def __init__(self):
        self.steps, self.group_of, self.groups = {}, {}, {}

    def work(self, key, needs, cost, run):
        self.steps[key] = (tuple(needs), cost, run, None, 0.0)

    def copy(self, key, needs, rows, src, dst, to, group=None):
        links, times, more = ROUTE[to]
        length = rows * times * (CORE_ROW if to == "core" else LINK_ROW)
        wait = CORE_WAIT if to == "core" else LINK_WAIT + more
        self.steps[key] = (tuple(needs), length, (src, dst, to), links, wait)
        self.group_of[key] = group or key
        self.groups.setdefault(group or key, []).append(key)

    def all_needs(self, key):
        result = []
        for need in self.steps[key][0]:
            result += self.groups[self.group_of[need]] if need in self.group_of else [need]
        return tuple(dict.fromkeys(result))

    def order(self):
        steps = {key: (self.all_needs(key), *step[1:]) for key, step in self.steps.items()}
        users = {key: [] for key in steps}
        for key, step in steps.items():
            for need in step[0]:
                users[need].append(key)
        left = {}

        def to_end(key):
            if key not in left:
                left[key] = steps[key][1] + steps[key][4] + max([to_end(user) for user in users[key]], default=0.0)
            return left[key]

        rank = {key: (-to_end(key), number) for number, key in enumerate(steps)}
        now, ready, free, end, result = 0.0, {}, {}, {}, []
        missing = {key: len(step[0]) for key, step in steps.items()}
        for key in steps:
            if not missing[key]:
                ready[key] = 0.0
        while ready:
            def opens(key):
                links = steps[key][3] or ()
                return max([ready[key]] + [free.get(link, 0.0) - QUEUE for link in links])

            now = max(now, min(opens(key) for key in ready))
            able = [key for key in ready if opens(key) <= now]
            key = min(able, key=lambda key: (steps[key][3] is None, rank[key]))
            del ready[key]
            needs, length, run, links, wait = steps[key]
            if links is None:
                now += length
                end[key] = now
            else:
                now += ISSUE
                for link in links:
                    free[link] = max(now, free.get(link, 0.0)) + length
                end[key] = max(free[link] for link in links) + wait
            result.append(key)
            for user in users[key]:
                missing[user] -= 1
                if not missing[user]:
                    ready[user] = max(end[need] for need in steps[user][0])
        return result, end


def kernel(
    img_in, txt_in, img_ids_in, txt_ids_in, scale_in, bias_in, img_out, txt_out,
    img_ref, txt_ref, img_ids_ref, txt_ids_ref, scale_ref, bias_ref, in_sems,
    imgs, txts, img_ids, txt_ids, img_col, txt_line, coef, img_part, txt_part,
    t1_send, t1_recv, t2_send, t2_recv, t3_send, t3_recv,
    core_send, core_recv, z_send, z_recv, send_sems, recv_sems,
):
    f32, bf16 = jnp.float32, jnp.bfloat16
    blk, grp = lax.axis_index("blk"), lax.axis_index("group")
    y, x_hi = lax.div(blk, 2), lax.rem(blk, 2)
    z, x_lo, core = lax.div(grp, 4), lax.rem(lax.div(grp, 2), 2), lax.rem(grp, 2)
    x = x_hi * 2 + x_lo

    def device(dx=0, dy=0, dz=0, dc=0):
        nx, ny, nz = lax.rem(x + dx + 4, 4), lax.rem(y + dy + 4, 4), lax.rem(z + dz + 8, 8)
        nc = lax.rem(core + dc, 2)
        return (ny * 2 + lax.div(nx, 2), (nz * 2 + lax.rem(nx, 2)) * 2 + nc)

    near = {
        "x+": device(dx=1), "x-": device(dx=-1), "y+": device(dy=1), "y-": device(dy=-1),
        "z+": device(dz=1), "z-": device(dz=-1), "core": device(dc=1),
        "x2": device(dx=2), "y2": device(dy=2), "z+2": device(dz=2), "z-2": device(dz=-2),
    }
    barrier = pltpu.get_barrier_semaphore()
    for there in near.values():
        pl.semaphore_signal(barrier, inc=1, device_id=there, device_id_type=MESH)

    loads = [
        pltpu.make_async_copy(src, dst, in_sems.at[number])
        for number, (src, dst) in enumerate([
            (img_in, img_ref), (txt_in, txt_ref), (img_ids_in, img_ids_ref), (txt_ids_in, txt_ids_ref),
            (scale_in, scale_ref), (bias_in, bias_ref),
        ])
    ]
    for load in loads:
        load.start()
    for load in loads:
        load.wait()
    own_img, own_txt = IMG_ROW[0, 0], {p: TXT_ROW[p, 0, 0] for p in "AB"}
    imgs[own_img:own_img + OWN, :] = unit_rows(img_ref[...])[0].astype(bf16)
    unit = unit_rows(txt_ref[...])[0].astype(bf16)
    txts[own_txt["A"]:own_txt["A"] + HALF, :] = unit[:HALF]
    txts[own_txt["B"]:own_txt["B"] + HALF, :] = unit[HALF:]
    line = img_ids_ref[...]
    img_ids[own_img // OWN] = jnp.concatenate([line] * 2, axis=1)
    line = txt_ids_ref[...]
    txt_ids[own_txt["A"] // HALF] = jnp.concatenate([line[:, :HALF]] * 4, axis=1)
    txt_ids[own_txt["B"] // HALF] = jnp.concatenate([line[:, HALF:]] * 4, axis=1)
    scale = jnp.exp(jnp.broadcast_to(scale_ref[...], (1, 256)))
    half_scale, half_bias = 0.5 * scale[:, 0:1], 0.5 * bias_ref[...]
    pl.semaphore_wait(barrier, len(near))

    plan = Plan()
    first_axis, second_axis = {"A": "x", "B": "y"}, {"A": "y", "B": "x"}
    halves = (0, 1)

    def move_text(p, src, dst, piece, to, needs):
        low = piece * QUART
        a, b = TXT_ROW[p, *src] + low, TXT_ROW[p, *dst] + low
        d, e = dst
        group = ("t", p, "far") if d == 2 else ("t", p, "rest") if (d == 1 and e > 1) or (d == 3 and e < 2) else None
        plan.copy(("t", p, *dst, piece), needs, QUART, txts.at[a:a + QUART, :], txts.at[b:b + QUART, :], to, group)

    def move_text_ids(p, src, dst, count, to, needs):
        a, b = TXT_ROW[p, *src] // HALF, TXT_ROW[p, *dst] // HALF
        group = {
            (0, 2): ("ti", p, 0), (0, 3): ("ti", p, 0), (2, 0): ("ti", p, 2), (2, 2): ("ti", p, 2),
            (1, 2): ("ti", p, "rest"), (3, 0): ("ti", p, "rest"),
        }.get(dst)
        plan.copy(("ti", p, *dst), needs, 1, txt_ids.at[a:a + count], txt_ids.at[b:b + count], to, group)

    def text_here(p, d, e, piece):
        return [] if (d, e) == (0, 0) else [("t", p, d, e, piece)]

    for p in "AB":
        one, two = first_axis[p], second_axis[p]
        for e, way, order in ((1, "+", (0, 1)), (3, "-", (1, 0))):
            for piece in order:
                move_text(p, (0, 0), (0, e), piece, one + way, [])
        for piece in halves:
            move_text(p, (0, 0), (0, 2), piece, one + "2", [])
        for e in range(4):
            for piece in halves:
                for d, way in ((1, "+"), (3, "-")):
                    move_text(p, (0, e), (d, e), piece, two + way, text_here(p, 0, e, piece))
                d, way = (1, "+") if e < 2 else (3, "-")
                move_text(p, (d, e), (2, e), piece, two + way, [("t", p, d, e, piece)])
        move_text_ids(p, (0, 0), (0, 1), 1, one + "+", [])
        move_text_ids(p, (0, 0), (0, 3), 1, one + "-", [])
        move_text_ids(p, (0, 0), (0, 2), 1, one + "2", [])
        for d, way in ((1, "+"), (3, "-")):
            move_text_ids(p, (0, 0), (d, 0), 2, two + way, [("ti", p, 0, 1)])
            move_text_ids(p, (0, 2), (d, 2), 2, two + way, [("ti", p, 0, 2), ("ti", p, 0, 3)])
        move_text_ids(p, (1, 0), (2, 0), 2, two + "+", [("ti", p, 1, 0)])
        move_text_ids(p, (3, 2), (2, 2), 2, two + "-", [("ti", p, 3, 2)])

    pieces = [(low, low + PIECE) for low in range(0, OWN, PIECE)]

    def move_image(src, dst, low, high, to, needs):
        a, b = IMG_ROW[src, 0], IMG_ROW[dst, 0]
        group = ("z", 4, "half", low // HALF) if dst == 4 else None
        plan.copy(
            ("z", dst, low), needs, high - low, imgs.at[a + low:a + high, :], imgs.at[b + low:b + high, :], to, group
        )

    for way, step in (("+", 1), ("-", -1)):
        for hops in range(1, 5):
            src, dst = (hops - 1 - hops // 4) * step % 8, hops * step % 8
            to = "z" + way + ("2" if hops == 4 else "")
            for low, high in pieces[::step]:
                if hops < 4 or (low < HALF) == (step > 0):
                    move_image(src, dst, low, high, to, [("z", src, low)] if src else [])
            if hops < 4 or step > 0:
                plan.copy(
                    ("zi", dst), [("zi", src)] if src else [], 1,
                    img_ids.at[IMG_ROW[src, 0] // OWN], img_ids.at[IMG_ROW[dst, 0] // OWN], to,
                )
    for dz in range(8):
        a, b = IMG_ROW[dz, 0], IMG_ROW[dz, 1]
        pair = min(dz, 8 - dz) or 1
        for half in halves:
            low, high = half * HALF, half * HALF + HALF
            plan.copy(
                ("c", dz, half), [("z", dz, at) for at, _ in pieces if low <= at < high and dz], HALF,
                imgs.at[a + low:a + high, :], imgs.at[b + low:b + high, :], "core", ("c", pair),
            )
        plan.copy(
            ("ci", dz), [("zi", dz)] if dz else [], 1, img_ids.at[a // OWN], img_ids.at[b // OWN], "core",
            ("ci", pair),
        )

    lane = lax.broadcasted_iota(jnp.int32, (1, 128), 1)

    def line_of_text(base):
        line = None
        for e in range(4):
            ids = txt_ids[base // HALF + e]
            line = ids if line is None else jnp.where(lane < HALF * e, line, ids)
        txt_line[:, base:base + 128] = line

    for base in range(0, ROWS, 128):
        ids = []
        for p, d, e in TXT_ORDER[base // HALF:base // HALF + 4]:
            if (d, e) != (0, 0):
                ids.append(("ti", p, d, e if d == 0 else e // 2 * 2))
        plan.work(("line", base), ids, 0.05, functools.partial(line_of_text, base))

    def column_of_images(row):
        place = row // OWN
        line = jnp.where(lane < OWN, img_ids[place], img_ids[place + 1])
        img_col[row:row + 128, :] = jnp.transpose(jnp.broadcast_to(line, (128, 128)))

    for row in range(0, ROWS, 128):
        ids = []
        for dz, cr in IMG_ORDER[row // OWN:row // OWN + 2]:
            ids += [("ci", dz)] if cr else [("zi", dz)] if dz else []
        plan.work(("column", row), ids, 0.1, functools.partial(column_of_images, row))

    def score_tile(r, high, t, right):
        scores = lax.dot_general(
            imgs[r:high, :], txts[t:right, :], (((1,), (1,)), ((), ())), preferred_element_type=f32
        )
        column = img_col[r:high, :]
        same = jnp.concatenate([column] * ((right - t) // 128), axis=1) == txt_line[:, t:right]
        value = 0.5 * jnp.tanh(half_scale * scores + half_bias) + jnp.where(same, -0.5, 0.5)
        coef[r:high, t:right] = value.astype(bf16)

    score_keys = []
    for r, high, t, right in SCORE_TILES:
        needs = [("column", row) for row in range(r, high, 128)] + [("line", base) for base in range(t, right, 128)]
        for dz, cr in IMG_ORDER[r // OWN:high // OWN]:
            needs += [("c", dz, half) for half in halves] if cr else [("z", dz, at) for at, _ in pieces if dz]
        for p, d, e in TXT_ORDER[t // HALF:right // HALF]:
            needs += [at for piece in halves for at in text_here(p, d, e, piece)]
        key = ("score", r, high, t, right)
        score_keys.append(key)
        cost = 0.08 + max(0.15, 0.0006 * (high - r)) * (right - t) / 256
        plan.work(key, needs, cost, functools.partial(score_tile, r, high, t, right))

    def img_terms(row):
        img_part[row:row + 128, :] = jnp.dot(coef[row:row + 128, :], txts[...], preferred_element_type=f32)

    def txt_terms(row):
        txt_part[row:row + 128, :] = lax.dot_general(
            coef[:, row:row + 128], imgs[...], (((0,), (0,)), ((), ())), preferred_element_type=f32
        )

    for row in range(0, ROWS, 128):
        needs = [key for key in score_keys if key[1] <= row < key[2]]
        plan.work(("img", row), needs, 0.41, functools.partial(img_terms, row))
        needs = [key for key in score_keys if key[3] <= row < key[4]]
        plan.work(("txt", row), needs, 0.42, functools.partial(txt_terms, row))

    def img_key(dz, cr):
        return ("img", IMG_ROW[dz, cr] // 128 * 128)

    def to_core(dz):
        row = IMG_ROW[dz, 1]
        core_send[OWN * dz:OWN * dz + OWN, :] = img_part[row:row + OWN, :].astype(bf16)

    def chip_sum(dz, low, high):
        row = IMG_ROW[dz, 0]
        return img_part[row + low:row + high, :] + core_recv[OWN * dz + low:OWN * dz + high, :].astype(f32)

    def z_out(dz, low, high, before):
        total = chip_sum(dz, low, high)
        for other in before:
            total = total + z_recv[OWN * other + low:OWN * other + high, :].astype(f32)
        z_send[OWN * dz + low:OWN * dz + high, :] = total.astype(bf16)

    for dz in range(8):
        rows = slice(OWN * dz, OWN * dz + OWN)
        plan.work(("to core", dz), [img_key(dz, 1)], 0.04, functools.partial(to_core, dz))
        plan.copy(("s", dz), [("to core", dz)], OWN, core_send.at[rows], core_recv.at[rows], "core", ("s", min(dz, 8 - dz)))
    for dz in (4, 3, 5, 2, 6, 1, 7):
        for low, high in pieces:
            way = "-" if dz < 4 or dz == 4 and low < HALF else "+"
            before = []
            if dz in (1, 2, 6, 7):
                before.append(dz + 1 if dz < 4 else dz - 1)
            if dz in (2, 6) and (low < HALF) == (dz == 2):
                before.append(4)
            needs = [img_key(dz, 0), ("s", dz)] + [("r", other, low) for other in before]
            plan.work(("z out", dz, low), needs, 0.03, functools.partial(z_out, dz, low, high, before))
            rows = slice(OWN * dz + low, OWN * dz + high)
            plan.copy(
                ("r", dz, low), [("z out", dz, low)], high - low, z_send.at[rows], z_recv.at[rows],
                "z" + way + ("2" if dz == 4 else ""),
                ("r", 1, "half", low // HALF) if dz in (1, 7) else None,
            )

    def t1_out(p, e, low, high):
        base, at = TXT_ROW[p, 2, e], 128 * "AB".index(p) + HALF * e
        t1_send[at + low:at + high, :] = txt_part[base + low:base + high, :].astype(bf16)

    def t2_out(p, d, e, low, high, added):
        base, at = TXT_ROW[p, d, e], 256 * "AB".index(p) + 128 * (d // 2) + HALF * e
        total = txt_part[base + low:base + high, :]
        if added:
            got = 128 * "AB".index(p) + HALF * e
            total = total + t1_recv[got + low:got + high, :].astype(f32)
        t2_send[at + low:at + high, :] = total.astype(bf16)

    def line_sum(p, e, low=0, high=HALF):
        base, at = TXT_ROW[p, 0, e], 256 * "AB".index(p) + HALF * e
        return (
            txt_part[base + low:base + high, :]
            + t2_recv[at + low:at + high, :].astype(f32)
            + t2_recv[at + 128 + low:at + 128 + high, :].astype(f32)
        )

    def t3_out(p, e, low, high):
        at = 96 * "AB".index(p) + HALF * (e - 1)
        t3_send[at + low:at + high, :] = line_sum(p, e, low, high).astype(bf16)

    def txt_key(p, d, e):
        return ("txt", TXT_ROW[p, d, e] // 128 * 128)

    def line_needs(p, e, low):
        return [txt_key(p, 0, e), ("t2", p, 1, e, low), ("t2", p, 3, e, low)]

    for p in "AB":
        one, two = first_axis[p], second_axis[p]
        for e in range(4):
            for low in (0, QUART):
                high = low + QUART
                at = 128 * "AB".index(p) + HALF * e
                rows = slice(at + low, at + high)
                plan.work(("t1 out", p, e, low), [txt_key(p, 2, e)], 0.02, functools.partial(t1_out, p, e, low, high))
                plan.copy(
                    ("t1", p, e, low), [("t1 out", p, e, low)], QUART, t1_send.at[rows], t1_recv.at[rows],
                    two + ("-" if e < 2 else "+"),
                )
                for d, way in ((1, "-"), (3, "+")):
                    added = (d == 1) == (e < 2)
                    at = 256 * "AB".index(p) + 128 * (d // 2) + HALF * e
                    rows = slice(at + low, at + high)
                    needs = [txt_key(p, d, e)] + ([("t1", p, e, low)] if added else [])
                    plan.work(
                        ("t2 out", p, d, e, low), needs, 0.03, functools.partial(t2_out, p, d, e, low, high, added)
                    )
                    plan.copy(
                        ("t2", p, d, e, low), [("t2 out", p, d, e, low)], QUART, t2_send.at[rows], t2_recv.at[rows],
                        two + way, ("t2", p, e, low),
                    )
                if e:
                    at = 96 * "AB".index(p) + HALF * (e - 1)
                    rows = slice(at + low, at + high)
                    plan.work(
                        ("t3 out", p, e, low), line_needs(p, e, low), 0.03, functools.partial(t3_out, p, e, low, high)
                    )
                    plan.copy(
                        ("t3", p, e, low), [("t3 out", p, e, low)], QUART, t3_send.at[rows], t3_recv.at[rows],
                        one + " -2+"[e], ("t3", p),
                    )

    def finish(embedding, total):
        unit, inverse = unit_rows(embedding)
        direction = scale[:, 0:1] * total
        return inverse * (direction - unit * jnp.sum(unit * direction, axis=1, keepdims=True))

    def finish_txt(p):
        low = HALF * "AB".index(p)
        total = line_sum(p, 0)
        for e in (1, 2, 3):
            at = 96 * "AB".index(p) + HALF * (e - 1)
            total = total + t3_recv[at:at + HALF, :].astype(f32)
        txt_out[low:low + HALF, :] = finish(txt_ref[low:low + HALF, :], total)

    def finish_img(low, high):
        total = chip_sum(0, low, high)
        for dz in (1, 7):
            total = total + z_recv[OWN * dz + low:OWN * dz + high, :].astype(f32)
        img_out[low:high, :] = finish(img_ref[low:high, :], total)

    for p in "AB":
        needs = [need for low in (0, QUART) for need in line_needs(p, 0, low) + [("t3", p, e, low) for e in (1, 2, 3)]]
        plan.work(("end", p), needs, 0.2, functools.partial(finish_txt, p))
    for low in (HALF, 0):
        needs = [img_key(0, 0), ("s", 0), ("r", 1, low)]
        plan.work(("end", low), needs, 0.15, functools.partial(finish_img, low, low + HALF))

    arrives = {group: recv_sems.at[number] for number, group in enumerate(plan.groups)}
    sent = []

    def whole(rows, ids):
        return txt_ids.at[0:rows] if ids else imgs.at[0:rows, :]

    def await_copy(ref, sem):
        pltpu.make_async_copy(ref, ref, sem).wait()

    here = set()
    for key in plan.order()[0]:
        needs, _, run, links, _ = plan.steps[key]
        for need in needs:
            group = plan.group_of.get(need)
            if group is None or group in here:
                continue
            here.add(group)
            landed = [plan.steps[member][2][1] for member in plan.groups[group]]
            ids = landed[0].dtype != bf16
            await_copy(whole(sum(1 if ref.ndim == 2 and ids else ref.shape[0] for ref in landed), ids), arrives[group])
        if links is None:
            run()
            continue
        src, dst, to = run
        ids = src.dtype != bf16
        rows = 1 if src.ndim == 2 and ids else src.shape[0]
        open_sems = [entry for entry in sent if entry[0] == ids and entry[1] + rows <= (32 if ids else ROWS)]
        if not open_sems:
            open_sems = [[ids, 0, send_sems.at[len(sent)]]]
            sent.append(open_sems[0])
        open_sems[0][1] += rows
        pltpu.make_async_remote_copy(
            src_ref=src, dst_ref=dst, send_sem=open_sems[0][2], recv_sem=arrives[plan.group_of[key]],
            device_id=near[to], device_id_type=MESH,
        ).start()
    for ids, rows, sem in sent:
        await_copy(whole(rows, ids), sem)


def write_out(img_grad, txt_grad, img_out, txt_out, sems):
    copies = [
        pltpu.make_async_copy(src.at[low:low + QUART], dst.at[low:low + QUART], sems.at[side, low // QUART])
        for low in range(0, OWN, QUART)
        for side, (src, dst) in enumerate([(img_grad, img_out), (txt_grad, txt_out)])
    ]
    for copy in copies:
        copy.start()
    for copy in copies:
        copy.wait()


def body(img_emb, txt_emb, img_ids, txt_ids, scale_logarithm, bias):
    f32, bf16, i32 = jnp.float32, jnp.bfloat16, jnp.int32
    anywhere = pl.BlockSpec(memory_space=pl.ANY)
    in_vmem = pl.BlockSpec(memory_space=pltpu.VMEM)
    grads = pl.pallas_call(
        kernel,
        out_shape=(pltpu.VMEM((OWN, D), f32), pltpu.VMEM((OWN, D), f32)),
        in_specs=[anywhere] * 6,
        out_specs=(in_vmem, in_vmem),
        scratch_shapes=[
            pltpu.VMEM((OWN, D), bf16),
            pltpu.VMEM((OWN, D), bf16),
            pltpu.VMEM((1, OWN), i32),
            pltpu.VMEM((1, OWN), i32),
            pltpu.VMEM((1, 1), f32),
            pltpu.VMEM((1, 1), f32),
            pltpu.SemaphoreType.DMA((6,)),
            pltpu.VMEM((ROWS, D), bf16),
            pltpu.VMEM((ROWS, D), bf16),
            pltpu.VMEM((16, 1, 128), i32),
            pltpu.VMEM((32, 1, 128), i32),
            pltpu.VMEM((ROWS, 128), i32),
            pltpu.VMEM((1, ROWS), i32),
            pltpu.VMEM((ROWS, ROWS), bf16),
            pltpu.VMEM((ROWS, D), f32),
            pltpu.VMEM((ROWS, D), f32),
            pltpu.VMEM((256, D), bf16),
            pltpu.VMEM((256, D), bf16),
            pltpu.VMEM((512, D), bf16),
            pltpu.VMEM((512, D), bf16),
            pltpu.VMEM((192, D), bf16),
            pltpu.VMEM((192, D), bf16),
            pltpu.VMEM((512, D), bf16),
            pltpu.VMEM((512, D), bf16),
            pltpu.VMEM((512, D), bf16),
            pltpu.VMEM((512, D), bf16),
            pltpu.SemaphoreType.DMA((N_SENT,)),
            pltpu.SemaphoreType.DMA((N_ARRIVALS,)),
        ],
        compiler_params=pltpu.CompilerParams(
            collective_id=0, has_side_effects=True, vmem_limit_bytes=56 * 1024 * 1024
        ),
        cost_estimate=pl.CostEstimate(flops=7247757312, bytes_accessed=900000, transcendentals=1048576),
    )(img_emb, txt_emb, img_ids.reshape(1, OWN), txt_ids.reshape(1, OWN),
      scale_logarithm.reshape(1, 1), bias.reshape(1, 1))
    return pl.pallas_call(
        write_out,
        out_shape=(jax.ShapeDtypeStruct((OWN, D), f32), jax.ShapeDtypeStruct((OWN, D), f32)),
        in_specs=[in_vmem, in_vmem],
        out_specs=(anywhere, anywhere),
        scratch_shapes=[pltpu.SemaphoreType.DMA((2, OWN // QUART))],
    )(*[pltpu.with_memory_space_constraint(grad, pltpu.VMEM) for grad in grads])


def solution(mesh):
    split = P(("blk", "group"), None)
    ids = P(("blk", "group"))
    return jax.shard_map(
        body,
        mesh=mesh,
        in_specs=(split, split, ids, ids, P(), P()),
        out_specs=(split, split),
        check_vma=False,
    )
```
